512 devices in a mesh: cuts: 2 (over y_lo), dp: 16 (over z), row: 4 (over y_hi, core), col: 4 (over x).
Axes of the slice: x: 4, y: 4 (y_hi: 2, y_lo: 2; y = y_hi * 2 + y_lo), z: 16, core: 2. Of those that a mesh axis runs over, the one named last changes fastest.
Arguments:
- tokens: bfloat16 [32768, 4096], P(('cuts', 'dp'), 'row'), may hold values from -6 to 6
- cotangent: bfloat16 [32768, 4096], P(('cuts', 'dp'), 'col'), may hold values from -0.03125 to 0.03125
- norm_gain: float32 [4096], P('row'), may hold values from 0.5 to 6
- row_prev: float32 [4, 1024], P('row', 'dp'), may hold values from 0.02 to 0.5
- col_prev: float32 [4096], P('col'), may hold values from 0.002 to 0.05
Outputs:
- update: float32 [4, 1024, 4096], P('row', 'dp', 'col')
- row_moment: float32 [4, 1024], P('row', 'dp')
- col_moment: float32 [4096], P('col')
The draws below stay inside these ranges and needn't reach their ends.
All inputs are finite; a program needn't handle non-finite values.
Results may differ from the reference program's by a relative error of at most 0.0004.
Values sent between devices are 32-bit elements; how exact they have to be, the bound alone decides.
A program may use at most 64 MiB of HBM per device.

```python
import math
import jax
import jax.numpy as jnp
from jax import lax

D = 4096
TOK_DEV = 1024
F = 4096
TOKENS = 32768
SLABS = 4
SLAB_ROWS = 1024
N_CUTS = 2
N_DP = 16


def draw_norm_gain(key, part):
    position = jnp.arange(D, dtype=jnp.float32) / (D - 1)
    trend = jnp.power(3.0, position)
    noise = jnp.exp(jax.random.uniform(key, (D,), jnp.float32, -0.69, 0.69))
    return trend * noise


def levels(stream_key, extent, pieces, least, high):
    gain = 1.0
    for axis_at, blocks in pieces:
        heights = jax.random.uniform(jax.random.fold_in(jax.random.fold_in(stream_key, 6), axis_at), (blocks,), jnp.float32, least / len(pieces), high / len(pieces))
        gain = gain * jnp.repeat(jnp.exp(heights), extent[axis_at] // blocks).reshape((-1,) + (1,) * (len(extent) - 1 - axis_at))
    return gain


def bell_draw(own_key, dims, width, reach, cuts=(), kind=jnp.bfloat16):
    result = jax.random.normal(own_key, dims, jnp.float32) * width
    if len(cuts) > 0:
        result = levels(own_key, dims, cuts, -0.22, 0.18) * result
    return jnp.clip(result, min=-reach, max=reach).astype(kind)


def setup_inputs(seed: int = 0) -> dict:
    arg_keys = jax.random.split(jax.random.key(seed), 6)
    return {
        "tokens": bell_draw(arg_keys[0], (TOKENS, D), 1.0, 6.0, ((0, 32), (1, 4))),
        "cotangent": bell_draw(arg_keys[1], (TOKENS, F), TOKENS ** -0.5, 0.03125, ((0, 32), (1, 4))),
        "norm_gain": draw_norm_gain(jax.random.fold_in(arg_keys[5], 71), 0),
        "row_prev": jnp.clip(jnp.exp(math.log(0.5) - 3.218876 * jax.random.uniform(arg_keys[3], (SLABS, SLAB_ROWS), jnp.float32) ** levels(arg_keys[3], (SLABS, SLAB_ROWS), ((0, 4), (1, 16)), -0.2, 0.2)), 0.02, 0.5),
        "col_prev": jnp.clip(jnp.exp(math.log(0.05) - 3.218876 * jax.random.uniform(arg_keys[4], (F,), jnp.float32) ** levels(arg_keys[4], (F,), ((0, 4),), -0.2, 0.2)), 0.002, 0.05),
    }


decay_rate = 0.975
epsilon_one = 1e-30
clip_level = 1.0

def reference(tokens, cotangent, norm_gain, row_prev, col_prev):
    groups_count = N_CUTS * N_DP
    token_groups = tokens.reshape(groups_count, TOK_DEV, D)
    cot_groups = cotangent.reshape(groups_count, TOK_DEV, F)
    gradient = jnp.zeros((D, F), jnp.float32)
    for group in range(groups_count):
        product = jnp.dot(token_groups[group].T, cot_groups[group], preferred_element_type=jnp.float32)
        gradient = gradient + product * norm_gain[:, None]
    squares = gradient * gradient
    rows_prev = row_prev.reshape(D)
    row_moment = decay_rate * rows_prev + (1.0 - decay_rate) * (lax.optimization_barrier(jnp.sum(squares, axis=1)) / F + epsilon_one)
    col_moment = decay_rate * col_prev + (1.0 - decay_rate) * (lax.optimization_barrier(jnp.sum(squares, axis=0)) / D + epsilon_one)
    factor = row_moment[:, None] * col_moment[None, :]
    raw_update = gradient / jnp.sqrt(factor)
    clip_scale = jnp.maximum(1.0, jnp.sqrt(jnp.sum(raw_update * raw_update) / (D * F)) / clip_level)
    update = (raw_update / clip_scale).reshape(SLABS, SLAB_ROWS, F)
    return (update, row_moment.reshape(SLABS, SLAB_ROWS), col_moment)
```

```python
import jax
import jax.numpy as jnp
from jax import lax
from jax.experimental import pallas as pl
from jax.experimental.pallas import tpu as pltpu
from jax.sharding import PartitionSpec as P

MESH = pl.DeviceIdType.MESH
F32 = jnp.float32

D = 4096
F = 4096
DECAY = 0.975
EPS = 1e-30
CLIP = 1.0

NZ, NROW, NCOL, NCUT = 16, 4, 4, 2
N8 = NROW * NCUT
ROWS = 64
HALF = 32
WIDE = 1024
W = 256
ZF = 2 * W

Z_CHUNKS = [(0, 1, 0), (W, 1, 1), (0, 0, 0), (W, 0, 1)]
Y_CHUNKS = [(ZF, 0, 0), (ZF + W, 0, 1)]
CHUNKS = Z_CHUNKS + Y_CHUNKS
NCH = len(CHUNKS)


def kernel(
    x_hbm, c_hbm, gain_ref, rprev_ref, cprev_ref,
    upd_ref, rmom_ref, cmom_ref,
    x_ref, c_ref, part, rbuf, ybuf, zx_src, zx_dst, gfull,
    rr, rx_src, rx_dst, ab_src, ab, zab, fin,
    in_sem, ssem, rsem, ys, yr, zxs, zxr, gs, gr, rs, rrs, rxs, rxr, abs_, abr, zs, zr, fs, fr,
):
    d = lax.axis_index("dp")
    c = lax.axis_index("cuts")
    row = lax.axis_index("row")
    col = lax.axis_index("col")
    other = 1 - c
    me8 = row * NCUT + c
    me32 = col * N8 + me8
    up = {"dp": lax.rem(d + 1, NZ)}
    down = {"dp": lax.rem(d + NZ - 1, NZ)}
    pair = {"cuts": other}

    def peer8(k):
        e = lax.rem(me8 + k, N8)
        return e, {"row": e // NCUT, "cuts": lax.rem(e, NCUT)}

    def remote(src, dst, s, r, dev):
        return pltpu.make_async_remote_copy(
            src_ref=src, dst_ref=dst, send_sem=s, recv_sem=r,
            device_id=dev, device_id_type=MESH,
        )

    load_c = pltpu.make_async_copy(c_hbm, c_ref, in_sem.at[0])
    load_x = pltpu.make_async_copy(x_hbm, x_ref, in_sem.at[1])
    load_c.start()
    load_x.start()

    barrier = pltpu.get_barrier_semaphore()

    def greet(dev):
        pl.semaphore_signal(barrier, inc=1, device_id=dev, device_id_type=MESH)

    greet(up)
    greet(down)
    for k in range(1, N8):
        greet(peer8(k)[1])
    for k in range(1, NCOL):
        greet({"col": lax.rem(col + k, NCOL)})

    load_c.wait()
    load_x.wait()

    def product(j):
        half = (j + 1) // 2
        step = jnp.where(j % 2 == 1, half, -half)
        p = lax.rem(d // 2 + 4 + step + 8, 8)
        at = pl.ds(pl.multiple_of(p * 128, 128), 128)
        part[at, :] = lax.dot_general(
            x_ref[:, at], c_ref[...], (((0,), (0,)), ((), ())),
            preferred_element_type=F32,
        )
        return p

    def y_copy(e):
        rows_ = pl.ds(pl.multiple_of(e * ROWS + other * HALF, HALF), HALF)
        return remote(part.at[rows_, pl.ds(ZF, WIDE - ZF)], ybuf.at[e], ys.at[e], yr.at[e], pair)

    def y_send(j):
        half = (j + 1) // 2
        step = jnp.where(j % 2 == 1, half, -half)
        p = lax.rem(d // 2 + 4 + step + 8, 8)
        y_copy(2 * p).start()
        y_copy(2 * p + 1).start()

    def first(j, _):
        product(j)
        return 0

    def later(j, _):
        product(j)
        y_send(j)
        return 0

    lax.fori_loop(0, 3, first, 0)
    pl.semaphore_wait(barrier, 2 + (N8 - 1) + (NCOL - 1))

    def reach(direction, which):
        return 8 if direction == which else 7

    def own(e, chunk):
        start, theirs, _ = chunk
        h = other if theirs else c
        return part.at[
            pl.ds(pl.multiple_of(e * ROWS + h * HALF, HALF), HALF), pl.ds(start, W)
        ]

    def dest(direction, distance):
        if direction == 0:
            return lax.rem(d + distance, NZ)
        return lax.rem(d + NZ - distance, NZ)

    def hop(direction, n, i, src):
        ch = direction * NCH + n
        return remote(
            src, rbuf.at[ch, i], ssem.at[ch, i], rsem.at[ch, i], down if direction else up
        )

    def begin(direction, n, i):
        hop(direction, n, i, own(dest(direction, 8 - i), CHUNKS[n])).start()

    def forward(direction, n, i):
        ch = direction * NCH + n
        slot = rbuf.at[ch, i - 1]
        hop(direction, n, i - 1, slot).wait_recv()
        slot[...] += own(dest(direction, 8 - i), CHUNKS[n])[...]
        hop(direction, n, i, slot).start()

    def y_add(e):
        y_copy(e).wait_recv()
        rows_ = pl.ds(pl.multiple_of(e * ROWS + c * HALF, HALF), HALF)
        part[rows_, pl.ds(ZF, WIDE - ZF)] += ybuf[e]

    zn = range(len(Z_CHUNKS))
    yn = range(len(Z_CHUNKS), NCH)

    for n in zn:
        which = CHUNKS[n][2]
        begin(which, n, 0)
    for j in range(3):
        y_send(j)
    for n in zn:
        which = CHUNKS[n][2]
        begin(1 - which, n, 1)
    lax.fori_loop(3, 8, later, 0)

    def z_first(i):
        for n in zn:
            which = CHUNKS[n][2]
            forward(which, n, i)

    def z_step(i):
        for n in zn:
            for direction in (0, 1):
                forward(direction, n, i)

    def y_step(i):
        y_add(dest(0, 8 - i))
        y_add(dest(1, 8 - i))
        for n in yn:
            for direction in (0, 1):
                forward(direction, n, i)

    z_first(1)
    y_add(dest(0, 8))
    for n in yn:
        begin(CHUNKS[n][2], n, 0)
    y_add(dest(0, 7))
    y_add(dest(1, 7))
    for n in yn:
        begin(1 - CHUNKS[n][2], n, 1)
    for n in yn:
        forward(CHUNKS[n][2], n, 1)

    def steps(i, _):
        z_step(i)
        y_step(i)
        return 0

    lax.fori_loop(2, 8, steps, 0)

    lane = lax.broadcasted_iota(jnp.int32, (HALF, WIDE), 1)
    sub = lax.broadcasted_iota(jnp.int32, (HALF, WIDE), 0)
    gain = jnp.sum(
        jnp.where(lane == sub + d * ROWS + c * HALF, gain_ref[...], 0.0), axis=1, keepdims=True
    )

    def collect(n):
        for direction in (0, 1):
            hop(direction, n, 7, rbuf.at[direction * NCH + n, 7]).wait_recv()
        return own(d, CHUNKS[n])[...] + rbuf[n, 7] + rbuf[NCH + n, 7]

    for n in zn:
        start, theirs, _ = CHUNKS[n]
        if theirs:
            zx_src[:, pl.ds(start, W)] = collect(n)
    zx = remote(zx_src, zx_dst, zxs, zxr, pair)
    zx.start()
    y_add(d)
    mine = pl.ds(pl.multiple_of(c * HALF, HALF), HALF)
    for n in range(NCH):
        start, theirs, _ = CHUNKS[n]
        if not theirs:
            gfull[mine, pl.ds(start, W)] = collect(n)
    zx.wait_recv()
    gfull[mine, pl.ds(0, ZF)] += zx_dst[...]
    g = gfull[mine, :] * gain
    gfull[mine, :] = g
    g_copy = remote(gfull.at[mine], gfull.at[mine], gs, gr, pair)
    g_copy.start()

    lane1 = lax.broadcasted_iota(jnp.int32, (HALF, 128), 1)
    sub1 = lax.broadcasted_iota(jnp.int32, (HALF, 128), 0)
    diag = lane1 == sub1 + c * HALF
    sq = g * g
    rsum = jnp.sum(sq, axis=1, keepdims=True)
    rr[col] = jnp.sum(jnp.where(diag, rsum, 0.0), axis=0, keepdims=True)
    rcopies = []
    for k in range(1, NCOL):
        to = lax.rem(col + k, NCOL)
        cp = remote(rr.at[col], rr.at[col], rs.at[k], rrs.at[col], {"col": to})
        cp.start()
        rcopies.append(cp)
    asum = jnp.sum(sq, axis=0, keepdims=True)
    for e in range(N8):
        ab_src[e, :, pl.ds(0, 128)] = asum[:, e * 128:(e + 1) * 128]
    for k in range(1, NCOL):
        frm = lax.rem(col + k, NCOL)
        remote(rr.at[frm], rr.at[frm], rs.at[k], rrs.at[frm], {"col": frm}).wait_recv()
    total = rr[0] + rr[1] + rr[2] + rr[3]
    lane_r = lax.broadcasted_iota(jnp.int32, (1, 128), 1)
    in_half = (lane_r >= c * HALF) & (lane_r < c * HALF + HALF)
    rprev = jnp.concatenate([rprev_ref[...], rprev_ref[...]], axis=1)
    rmom = DECAY * rprev + (1.0 - DECAY) * (total / F + EPS)
    rmom = jnp.where(in_half, rmom, 0.0)
    rx_src[...] = rmom
    rx = remote(rx_src, rx_dst, rxs, rxr, pair)
    rx.start()
    rcol = jnp.sum(jnp.where(diag, rmom, 0.0), axis=1, keepdims=True)
    bsum = jnp.sum(sq * (1.0 / rcol), axis=0, keepdims=True)
    for e in range(N8):
        ab_src[e, :, pl.ds(128, 128)] = bsum[:, e * 128:(e + 1) * 128]

    acopies = []
    for k in range(1, N8):
        e, dev = peer8(k)
        cp = remote(ab_src.at[e], ab.at[me8], abs_.at[k], abr.at[me8], dev)
        cp.start()
        acopies.append(cp)
    ab[me8] = ab_src[me8]
    for k in range(1, N8):
        e, dev = peer8(k)
        remote(ab_src.at[e], ab.at[e], abs_.at[k], abr.at[e], dev).wait_recv()
    acc = ab[0]
    for e in range(1, N8):
        acc = acc + ab[e]

    zab[d] = acc
    zcopies = []
    for k in range(1, NZ):
        to = lax.rem(d + k, NZ)
        cp = remote(zab.at[d], zab.at[d], zs.at[k], zr.at[d], {"dp": to})
        cp.start()
        zcopies.append(cp)
    cprev = cprev_ref[:, pl.ds(pl.multiple_of(me8 * 128, 128), 128)]
    for k in range(1, NZ):
        frm = lax.rem(d + k, NZ)
        remote(zab.at[frm], zab.at[frm], zs.at[k], zr.at[frm], {"dp": frm}).wait_recv()
    acc = zab[0]
    for e in range(1, NZ):
        acc = acc + zab[e]
    cmom = DECAY * cprev + (1.0 - DECAY) * (acc[:, 0:128] / D + EPS)
    fin[me32, :, pl.ds(0, 128)] = cmom
    fin[me32, :, pl.ds(128, 128)] = acc[:, 128:256] / cmom

    def plane(k):
        e = lax.rem(me32 + k, NCOL * N8)
        return e, {
            "col": e // N8,
            "row": lax.rem(e, N8) // NCUT,
            "cuts": lax.rem(e, NCUT),
        }

    fcopies = []
    for k in range(1, NCOL * N8):
        _, dev = plane(k)
        cp = remote(fin.at[me32], fin.at[me32], fs.at[k], fr.at[me32], dev)
        cp.start()
        fcopies.append(cp)

    rx.wait_recv()
    rfull = rmom + rx_dst[...]
    rmom_ref[...] = rfull[:, 0:ROWS]
    lane2 = lax.broadcasted_iota(jnp.int32, (ROWS, 128), 1)
    sub2 = lax.broadcasted_iota(jnp.int32, (ROWS, 128), 0)
    rscale = lax.rsqrt(jnp.sum(jnp.where(lane2 == sub2, rfull, 0.0), axis=1, keepdims=True))
    g_copy.wait_recv()

    for k in range(1, NCOL * N8):
        e, dev = plane(k)
        remote(fin.at[e], fin.at[e], fs.at[k], fr.at[e], dev).wait_recv()
    tot = fin[0, :, pl.ds(128, 128)]
    for e in range(1, NCOL * N8):
        tot = tot + fin[e, :, pl.ds(128, 128)]
    ratio = jnp.sum(tot, axis=1, keepdims=True) / (D * F)
    inverse = 1.0 / jnp.maximum(1.0, jnp.sqrt(ratio) / CLIP)
    rows_scale = rscale * inverse
    for e in range(N8):
        at = pl.ds(e * 128, 128)
        cm = fin[col * N8 + e, :, pl.ds(0, 128)]
        cmom_ref[:, at] = cm
        upd_ref[:, at] = gfull[:, at] * rows_scale * lax.rsqrt(cm)

    for n in range(NCH):
        for direction in (0, 1):
            ch = direction * NCH + n
            lo = 0 if direction == CHUNKS[n][2] else 1

            def drain(i, _, direction=direction, n=n, ch=ch):
                hop(direction, n, i, rbuf.at[ch, i]).wait_send()
                return 0

            lax.fori_loop(lo, 8, drain, 0)

    def drain_y(e, _):
        y_copy(e).wait_send()
        return 0

    lax.fori_loop(0, NZ, drain_y, 0)
    zx.wait_send()
    g_copy.wait_send()
    rx.wait_send()
    for cp in rcopies + acopies + zcopies + fcopies:
        cp.wait_send()


def body(tokens, cotangent, norm_gain, row_prev, col_prev):
    vmem = pl.BlockSpec(memory_space=pltpu.VMEM)
    hbm = pl.BlockSpec(memory_space=pl.ANY)
    dma = pltpu.SemaphoreType.DMA
    update, row_moment, col_moment = pl.pallas_call(
        kernel,
        out_shape=(
            jax.ShapeDtypeStruct((ROWS, WIDE), F32),
            jax.ShapeDtypeStruct((1, ROWS), F32),
            jax.ShapeDtypeStruct((1, WIDE), F32),
        ),
        in_specs=[hbm, hbm, vmem, vmem, vmem],
        out_specs=(vmem, vmem, vmem),
        scratch_shapes=[
            pltpu.VMEM((1024, 1024), jnp.bfloat16),
            pltpu.VMEM((1024, 1024), jnp.bfloat16),
            pltpu.VMEM((1024, WIDE), F32),
            pltpu.VMEM((2 * NCH, 8, HALF, W), F32),
            pltpu.VMEM((NZ, HALF, WIDE - ZF), F32),
            pltpu.VMEM((HALF, ZF), F32),
            pltpu.VMEM((HALF, ZF), F32),
            pltpu.VMEM((ROWS, WIDE), F32),
            pltpu.VMEM((NCOL, 1, 128), F32),
            pltpu.VMEM((1, 128), F32),
            pltpu.VMEM((1, 128), F32),
            pltpu.VMEM((N8, 1, 256), F32),
            pltpu.VMEM((N8, 1, 256), F32),
            pltpu.VMEM((NZ, 1, 256), F32),
            pltpu.VMEM((NCOL * N8, 1, 256), F32),
            dma((2,)),
            dma((2 * NCH, 8)), dma((2 * NCH, 8)),
            dma((NZ,)), dma((NZ,)),
            dma, dma, dma, dma,
            dma((NCOL,)), dma((NCOL,)),
            dma, dma,
            dma((N8,)), dma((N8,)),
            dma((NZ,)), dma((NZ,)),
            dma((NCOL * N8,)), dma((NCOL * N8,)),
        ],
        compiler_params=pltpu.CompilerParams(
            collective_id=0, has_side_effects=True, vmem_limit_bytes=40 << 20
        ),
        name="adafactor",
    )(tokens, cotangent, norm_gain[None, :], row_prev, col_prev[None, :])
    return update[None], row_moment, col_moment[0]


def solution(mesh):
    return jax.shard_map(
        body,
        mesh=mesh,
        in_specs=(
            P(("cuts", "dp"), "row"),
            P(("cuts", "dp"), "col"),
            P("row"),
            P("row", "dp"),
            P("col"),
        ),
        out_specs=(P("row", "dp", "col"), P("row", "dp"), P("col")),
        check_vma=False,
    )
```

```python
import functools

import jax
import jax.numpy as jnp
from jax import lax
from jax.experimental import pallas as pl
from jax.experimental.pallas import tpu as pltpu
from jax.sharding import PartitionSpec as P

MESH = pl.DeviceIdType.MESH
F32 = jnp.float32

D = 4096
F = 4096
DECAY = 0.975
EPS = 1e-30
CLIP = 1.0

NZ, NROW, NCOL, NCUT = 16, 4, 4, 2
N8 = NROW * NCUT
N32 = NCOL * N8
ROWS = 64
HALF = 32
WIDE = 1024


def make_chunks(cfg):
    zf, zs, yk = cfg["zf"], cfg["zs"], cfg["ys"]
    z, y = [], []
    for theirs in (1, 0):
        for q in range(zs):
            z.append((0, theirs, 0, HALF, q * (zf // zs), zf // zs, (1 - theirs + q) % 2))
    yw = (WIDE - zf) // yk
    for q in range(yk):
        for r in range(2):
            y.append((1, 0, r * 16, 16, zf + q * yw, yw, (r + q) % 2))
    return z, y


def kernel(cfg, *refs):
    zc, yc = make_chunks(cfg)
    chunks = zc + yc
    nch = len(chunks)
    zf = cfg["zf"]
    (x_hbm, c_hbm, gain_hbm, rprev_hbm, cprev_hbm, upd_ref, rmom_ref, cmom_ref,
     x_ref, c_ref, gain_ref, rprev_ref, cprev_ref, part) = refs[:14]
    rbufs = refs[14:14 + nch]
    (ybuf, zx_src, zx_dst, gfull, rr, rx_src, rx_dst, ab_src, ab, zab, fin,
     in_sem, ssem, rsem, ys, yr, zxs, zxr, gs, gr, rs, rrs, rxs, rxr, abs_, abr, zs, zr, fs, fr,
     ) = refs[14 + nch:]
    d = lax.axis_index("dp")
    c = lax.axis_index("cuts")
    row = lax.axis_index("row")
    col = lax.axis_index("col")
    other = 1 - c
    me8 = row * NCUT + c
    me32 = col * N8 + me8
    up = {"dp": lax.rem(d + 1, NZ)}
    down = {"dp": lax.rem(d + NZ - 1, NZ)}
    pair = {"cuts": other}

    def peer8(k):
        e = lax.rem(me8 + k, N8)
        return e, {"row": e // NCUT, "cuts": lax.rem(e, NCUT)}

    def remote(src, dst, s, r, dev):
        return pltpu.make_async_remote_copy(
            src_ref=src, dst_ref=dst, send_sem=s, recv_sem=r,
            device_id=dev, device_id_type=MESH,
        )

    barrier = pltpu.get_barrier_semaphore()

    def greet(dev):
        pl.semaphore_signal(barrier, inc=1, device_id=dev, device_id_type=MESH)

    def upper(j):
        return lax.rem(j + d, 2)

    def block(j):
        return lax.rem(d // 2 + 12 + (1 - 2 * upper(j)) * ((j + 1) // 2), 8)

    def x_load(j):
        at = pl.ds(pl.multiple_of(block(j) * 128, 128), 128)
        return pltpu.make_async_copy(x_hbm.at[:, at], x_ref.at[:, at], in_sem.at[j])

    c_loads = [
        pltpu.make_async_copy(c_hbm.at[pl.ds(n * 256, 256)], c_ref.at[pl.ds(n * 256, 256)], in_sem.at[8 + n])
        for n in range(4)
    ]
    small_loads = [
        pltpu.make_async_copy(a, b, in_sem.at[12 + n])
        for n, (a, b) in enumerate([
            (gain_hbm, gain_ref), (rprev_hbm, rprev_ref), (cprev_hbm, cprev_ref),
        ])
    ]
    x_load(0).start()
    for load in c_loads:
        load.start()
    for j in range(1, 8):
        x_load(j).start()
    for load in small_loads:
        load.start()
    greet(up)
    greet(down)
    for k in range(1, N8):
        greet(peer8(k)[1])
    for k in range(1, NCOL):
        greet({"col": lax.rem(col + k, NCOL)})
    for load in c_loads:
        load.wait()

    def product(j):
        at = pl.ds(pl.multiple_of(block(j) * 128, 128), 128)
        x_load(j).wait()
        part[at, :] = lax.dot_general(
            x_ref[:, at], c_ref[...], (((0,), (0,)), ((), ())),
            preferred_element_type=F32,
        )

    def y_copy(e):
        rows_ = pl.ds(pl.multiple_of(e * ROWS + other * HALF, HALF), HALF)
        return remote(part.at[rows_, pl.ds(zf, WIDE - zf)], ybuf.at[e], ys.at[e], yr.at[e], pair)

    def y_send(j):
        p = block(j)
        y_copy(2 * p + upper(j)).start()
        y_copy(2 * p + 1 - upper(j)).start()

    def first(j, _):
        product(j)
        return 0

    def later(j, _):
        product(j)
        y_send(j)
        return 0

    def own(e, chunk):
        _, theirs, r0, nr, c0, w, _ = chunk
        h = other if theirs else c
        return part.at[pl.ds(pl.multiple_of(e * ROWS + h * HALF + r0, nr), nr), pl.ds(c0, w)]

    def dest(direction, distance):
        return lax.rem(d + (NZ - distance if direction else distance), NZ)

    def hop(direction, n, i, src):
        ch = direction * nch + n
        return remote(
            src, rbufs[n].at[direction, i], ssem.at[ch, i], rsem.at[ch, i],
            {"dp": dest(direction, 1)},
        )

    def begin(direction, n, i):
        hop(direction, n, i, own(dest(direction, 8 - i), chunks[n])).start()

    def forward(direction, n, i):
        slot = rbufs[n].at[direction, i - 1]
        hop(direction, n, i - 1, slot).wait_recv()
        slot[...] += own(dest(direction, 8 - i), chunks[n])[...]
        hop(direction, n, i, slot).start()

    def y_add(e):
        y_copy(e).wait_recv()
        rows_ = pl.ds(pl.multiple_of(e * ROWS + c * HALF, HALF), HALF)
        part[rows_, pl.ds(zf, WIDE - zf)] += ybuf[e]

    zn = range(len(zc))
    yn = range(len(zc), nch)

    def start0(which_n):
        for n in which_n:
            begin(chunks[n][6], n, 0)

    def start1(which_n):
        for n in which_n:
            begin(1 - chunks[n][6], n, 1)

    def second(which_n):
        for n in which_n:
            forward(chunks[n][6], n, 1)

    def z_step(i):
        for n in zn:
            for direction in (0, 1):
                forward(direction, n, i)

    def y_step(i):
        for direction in (0, 1):
            y_add(dest(direction, 8 - i))
        for n in yn:
            for direction in (0, 1):
                forward(direction, n, i)

    product(0)
    pl.semaphore_wait(barrier, 2 + (N8 - 1) + (NCOL - 1))
    start0(zn)
    y_send(0)

    def fill(j, _):
        product(j)
        y_send(j)

        @pl.when(j == 1)
        def _():
            start1(zn)

        @pl.when(j == 5)
        def _():
            second(zn)

        return 0

    lax.fori_loop(1, 8, fill, 0)
    for load in small_loads:
        load.wait()
    y_add(dest(0, 8))
    start0(yn)
    z_step(2)
    for direction in (0, 1):
        y_add(dest(direction, 7))
    start1(yn)
    second(yn)

    def steps(i, _):
        z_step(i)
        y_step(i - 1)
        return 0

    lax.fori_loop(3, 8, steps, 0)

    def collect(n):
        for direction in (0, 1):
            hop(direction, n, 7, rbufs[n].at[direction, 7]).wait_recv()
        return own(d, chunks[n])[...] + rbufs[n][0, 7] + rbufs[n][1, 7]

    for n in zn:
        _, theirs, r0, nr, c0, w, _ = chunks[n]
        if theirs:
            zx_src[:, pl.ds(c0, w)] = collect(n)
    zx = remote(zx_src, zx_dst, zxs, zxr, pair)
    zx.start()
    y_step(7)
    y_add(d)

    lane = lax.broadcasted_iota(jnp.int32, (HALF, WIDE), 1)
    sub = lax.broadcasted_iota(jnp.int32, (HALF, WIDE), 0)
    gain = jnp.sum(
        jnp.where(lane == sub + d * ROWS + c * HALF, gain_ref[...], 0.0), axis=1, keepdims=True
    )
    mine = pl.ds(pl.multiple_of(c * HALF, HALF), HALF)
    for n in zn:
        _, theirs, r0, nr, c0, w, _ = chunks[n]
        if not theirs:
            gfull[mine, pl.ds(c0, w)] = collect(n)
    zx.wait_recv()
    gfull[mine, pl.ds(0, zf)] += zx_dst[...]
    for n in yn:
        _, theirs, r0, nr, c0, w, _ = chunks[n]
        gfull[pl.ds(pl.multiple_of(c * HALF + r0, nr), nr), pl.ds(c0, w)] = collect(n)
    g = gfull[mine, :] * gain
    gfull[mine, :] = g
    g_copy = remote(gfull.at[mine], gfull.at[mine], gs, gr, pair)

    lane1 = lax.broadcasted_iota(jnp.int32, (HALF, 128), 1)
    sub1 = lax.broadcasted_iota(jnp.int32, (HALF, 128), 0)
    diag = lane1 == sub1 + c * HALF
    sq = g * g
    rsum = jnp.sum(sq, axis=1, keepdims=True)
    rr[col] = jnp.sum(jnp.where(diag, rsum, 0.0), axis=0, keepdims=True)
    rcopies = []
    for k in range(1, NCOL):
        to = lax.rem(col + k, NCOL)
        cp = remote(rr.at[col], rr.at[col], rs.at[k], rrs.at[col], {"col": to})
        cp.start()
        rcopies.append(cp)
    g_copy.start()
    asum = jnp.sum(sq, axis=0, keepdims=True)
    for e in range(N8):
        ab_src[e, :, pl.ds(0, 128)] = asum[:, e * 128:(e + 1) * 128]
    for k in range(1, NCOL):
        frm = lax.rem(col + k, NCOL)
        remote(rr.at[frm], rr.at[frm], rs.at[k], rrs.at[frm], {"col": frm}).wait_recv()
    total = rr[0] + rr[1] + rr[2] + rr[3]
    lane_r = lax.broadcasted_iota(jnp.int32, (1, 128), 1)
    in_half = (lane_r >= c * HALF) & (lane_r < c * HALF + HALF)
    rprev = jnp.concatenate([rprev_ref[...], rprev_ref[...]], axis=1)
    rmom = DECAY * rprev + (1.0 - DECAY) * (total / F + EPS)
    rmom = jnp.where(in_half, rmom, 0.0)
    rcol = jnp.sum(jnp.where(diag, rmom, 0.0), axis=1, keepdims=True)
    bsum = jnp.sum(sq * (1.0 / rcol), axis=0, keepdims=True)
    for e in range(N8):
        ab_src[e, :, pl.ds(128, 128)] = bsum[:, e * 128:(e + 1) * 128]

    acopies = []
    for k in range(1, N8):
        e, dev = peer8(k)
        cp = remote(ab_src.at[e], ab.at[me8], abs_.at[k], abr.at[me8], dev)
        cp.start()
        acopies.append(cp)
    rx_src[...] = rmom
    rx = remote(rx_src, rx_dst, rxs, rxr, pair)
    rx.start()
    ab[me8] = ab_src[me8]
    for k in range(1, N8):
        e, dev = peer8(k)
        remote(ab_src.at[e], ab.at[e], abs_.at[k], abr.at[e], dev).wait_recv()
    acc = ab[0]
    for e in range(1, N8):
        acc = acc + ab[e]

    zab[d] = acc
    zcopies = []
    order = [8] + [k for m in range(7, 0, -1) for k in (m, 16 - m)]
    for k in order:
        to = lax.rem(d + k, NZ)
        cp = remote(zab.at[d], zab.at[d], zs.at[k], zr.at[d], {"dp": to})
        cp.start()
        zcopies.append(cp)
    cprev = cprev_ref[:, pl.ds(pl.multiple_of(me8 * 128, 128), 128)]
    for k in reversed(order):
        frm = lax.rem(d + k, NZ)
        remote(zab.at[frm], zab.at[frm], zs.at[k], zr.at[frm], {"dp": frm}).wait_recv()
    acc = zab[0]
    for e in range(1, NZ):
        acc = acc + zab[e]
    cmom = DECAY * cprev + (1.0 - DECAY) * (acc[:, 0:128] / D + EPS)
    fin[me32, :, pl.ds(0, 128)] = cmom
    fin[me32, :, pl.ds(128, 128)] = acc[:, 128:256] / cmom

    def plane(k):
        e = lax.rem(me32 + k, N32)
        return e, {
            "col": e // N8,
            "row": lax.rem(e, N8) // NCUT,
            "cuts": lax.rem(e, NCUT),
        }

    fcopies = []
    for k in range(1, N32):
        _, dev = plane(k)
        cp = remote(fin.at[me32], fin.at[me32], fs.at[k], fr.at[me32], dev)
        cp.start()
        fcopies.append(cp)

    rx.wait_recv()
    rfull = rmom + rx_dst[...]
    rmom_ref[...] = rfull[:, 0:ROWS]
    lane2 = lax.broadcasted_iota(jnp.int32, (ROWS, 128), 1)
    sub2 = lax.broadcasted_iota(jnp.int32, (ROWS, 128), 0)
    rscale = lax.rsqrt(jnp.sum(jnp.where(lane2 == sub2, rfull, 0.0), axis=1, keepdims=True))
    g_copy.wait_recv()

    for n in range(nch):
        for direction in (0, 1):
            lo = 0 if direction == chunks[n][6] else 1

            def drain(i, _, direction=direction, n=n):
                hop(direction, n, i, rbufs[n].at[direction, i]).wait_send()
                return 0

            lax.fori_loop(lo, 8, drain, 0)

    def drain_y(e, _):
        y_copy(e).wait_send()
        return 0

    lax.fori_loop(0, NZ, drain_y, 0)
    zx.wait_send()
    g_copy.wait_send()
    rx.wait_send()
    for cp in rcopies + acopies + zcopies:
        cp.wait_send()

    for k in range(1, N32):
        e, dev = plane(k)
        remote(fin.at[e], fin.at[e], fs.at[k], fr.at[e], dev).wait_recv()
    tot = fin[0, :, pl.ds(128, 128)]
    for e in range(1, N32):
        tot = tot + fin[e, :, pl.ds(128, 128)]
    ratio = jnp.sum(tot, axis=1, keepdims=True) / (D * F)
    inverse = 1.0 / jnp.maximum(1.0, jnp.sqrt(ratio) / CLIP)
    rows_scale = rscale * inverse
    for e in range(N8):
        at = pl.ds(e * 128, 128)
        cm = fin[col * N8 + e, :, pl.ds(0, 128)]
        cmom_ref[:, at] = cm
        upd_ref[:, at] = gfull[:, at] * rows_scale * lax.rsqrt(cm)
    for cp in fcopies:
        cp.wait_send()


def call(cfg, cid, name, tokens, cotangent, norm_gain, row_prev, col_prev):
    zc, yc = make_chunks(cfg)
    chunks = zc + yc
    nch = len(chunks)
    zf = cfg["zf"]
    vmem = pl.BlockSpec(memory_space=pltpu.VMEM)
    hbm = pl.BlockSpec(memory_space=pl.ANY)
    dma = pltpu.SemaphoreType.DMA
    bf = jnp.bfloat16
    return pl.pallas_call(
        functools.partial(kernel, cfg),
        out_shape=(
            jax.ShapeDtypeStruct((ROWS, WIDE), F32),
            jax.ShapeDtypeStruct((1, ROWS), F32),
            jax.ShapeDtypeStruct((1, WIDE), F32),
        ),
        in_specs=[hbm] * 5,
        out_specs=(vmem, vmem, vmem),
        scratch_shapes=[
            pltpu.VMEM((1024, 1024), bf),
            pltpu.VMEM((1024, 1024), bf),
            pltpu.VMEM((1, 1024), F32),
            pltpu.VMEM((1, ROWS), F32),
            pltpu.VMEM((1, WIDE), F32),
            pltpu.VMEM((1024, WIDE), F32),
        ] + [pltpu.VMEM((2, 8, ch[3], ch[5]), F32) for ch in chunks] + [
            pltpu.VMEM((NZ, HALF, WIDE - zf), F32),
            pltpu.VMEM((HALF, zf), F32),
            pltpu.VMEM((HALF, zf), F32),
            pltpu.VMEM((ROWS, WIDE), F32),
            pltpu.VMEM((NCOL, 1, 128), F32),
            pltpu.VMEM((1, 128), F32),
            pltpu.VMEM((1, 128), F32),
            pltpu.VMEM((N8, 1, 256), F32),
            pltpu.VMEM((N8, 1, 256), F32),
            pltpu.VMEM((NZ, 1, 256), F32),
            pltpu.VMEM((N32, 1, 256), F32),
            dma((15,)),
            dma((2 * nch, 8)), dma((2 * nch, 8)),
            dma((NZ,)), dma((NZ,)),
            dma, dma, dma, dma,
            dma((NCOL,)), dma((NCOL,)),
            dma, dma,
            dma((N8,)), dma((N8,)),
            dma((NZ,)), dma((NZ,)),
            dma((N32,)), dma((N32,)),
        ],
        compiler_params=pltpu.CompilerParams(
            collective_id=cid, has_side_effects=True, vmem_limit_bytes=56 << 20
        ),
        name=name,
    )(tokens, cotangent, norm_gain[None, :], row_prev, col_prev[None, :])


def write(u, r, c, uo, ro, co, sem):
    copies = [
        pltpu.make_async_copy(a, b, sem.at[n]) for n, (a, b) in enumerate([(u, uo), (r, ro), (c, co)])
    ]
    for cp in copies:
        cp.start()
    for cp in copies:
        cp.wait()


def body(tokens, cotangent, norm_gain, row_prev, col_prev):
    vmem = pl.BlockSpec(memory_space=pltpu.VMEM)
    hbm = pl.BlockSpec(memory_space=pl.ANY)
    u, r, c = call(CFG, 0, "adafactor", tokens, cotangent, norm_gain, row_prev, col_prev)
    u, r, c = pl.pallas_call(
        write,
        out_shape=tuple(jax.ShapeDtypeStruct(a.shape, F32) for a in (u, r, c)),
        in_specs=[vmem] * 3,
        out_specs=(hbm,) * 3,
        scratch_shapes=[pltpu.SemaphoreType.DMA((3,))],
        name="write",
    )(u, r, c)
    return u[None], r, c[0]


CFG = {"zf": 512, "zs": 1, "ys": 1}


def solution(mesh):
    return jax.shard_map(
        body,
        mesh=mesh,
        in_specs=(
            P(("cuts", "dp"), "row"),
            P(("cuts", "dp"), "col"),
            P("row"),
            P("row", "dp"),
            P("col"),
        ),
        out_specs=(P("row", "dp", "col"), P("row", "dp"), P("col")),
        check_vma=False,
    )
```

```python
import functools

import jax
import jax.numpy as jnp
from jax import lax
from jax.experimental import pallas as pl
from jax.experimental.pallas import tpu as pltpu
from jax.sharding import PartitionSpec as P

MESH = pl.DeviceIdType.MESH
F32 = jnp.float32

D = 4096
F = 4096
DECAY = 0.975
EPS = 1e-30
CLIP = 1.0

NZ, NROW, NCOL, NCUT = 16, 4, 4, 2
N8 = NROW * NCUT
N32 = NCOL * N8
ROWS = 64
HALF = 32
WIDE = 1024


def make_chunks(cfg):
    zf, zs, yk = cfg["zf"], cfg["zs"], cfg["ys"]
    z, y = [], []
    for theirs in (1, 0):
        for q in range(zs):
            z.append((0, theirs, 0, HALF, q * (zf // zs), zf // zs, (1 - theirs + q) % 2))
    yw = (WIDE - zf) // yk
    for q in range(yk):
        for r in range(2):
            y.append((1, 0, r * 16, 16, zf + q * yw, yw, (r + q) % 2))
    return z, y


def kernel(cfg, *refs):
    zc, yc = make_chunks(cfg)
    chunks = zc + yc
    nch = len(chunks)
    zf = cfg["zf"]
    (x_hbm, c_hbm, gain_hbm, rprev_hbm, cprev_hbm, upd_ref, rmom_ref, cmom_ref,
     x_ref, c_ref, gain_ref, rprev_ref, cprev_ref, part) = refs[:14]
    rbufs = refs[14:14 + nch]
    (ybuf, zx_src, zx_dst, gfull, rr, rx_src, rx_dst, ab_src, ab, zab, fin,
     in_sem, ssem, rsem, ys, yr, zxs, zxr, gs, gr, rs, rrs, rxs, rxr, abs_, abr, zs, zr, fs, fr,
     ) = refs[14 + nch:]
    d = lax.axis_index("dp")
    c = lax.axis_index("cuts")
    row = lax.axis_index("row")
    col = lax.axis_index("col")
    other = 1 - c
    me8 = row * NCUT + c
    me32 = col * N8 + me8
    up = {"dp": lax.rem(d + 1, NZ)}
    down = {"dp": lax.rem(d + NZ - 1, NZ)}
    pair = {"cuts": other}

    rows4 = [lax.rem(row + k, NROW) for k in range(NROW)]
    cols4 = [lax.rem(col + k, NCOL) for k in range(NCOL)]
    cuts2 = [c, other]

    group = [
        (rows4[a] * NCUT + cuts2[b], {"row": rows4[a], "cuts": cuts2[b]})
        for a in range(NROW) for b in range(NCUT) if a or b
    ]
    plane = [
        (cols4[k] * N8 + rows4[a] * NCUT + cuts2[b], {"col": cols4[k], "row": rows4[a], "cuts": cuts2[b]})
        for k in (2, 1, 3, 0) for a in (2, 1, 3, 0) for b in (1, 0) if k or a or b
    ]

    def remote(src, dst, s, r, dev):
        return pltpu.make_async_remote_copy(
            src_ref=src, dst_ref=dst, send_sem=s, recv_sem=r,
            device_id=dev, device_id_type=MESH,
        )

    barrier = pltpu.get_barrier_semaphore()

    def greet(dev):
        pl.semaphore_signal(barrier, inc=1, device_id=dev, device_id_type=MESH)

    def upper(j):
        return lax.rem(j + d, 2)

    def block(j):
        return lax.rem(d // 2 + 12 + (1 - 2 * upper(j)) * ((j + 1) // 2), 8)

    def x_load(j):
        at = pl.ds(pl.multiple_of(block(j) * 128, 128), 128)
        return pltpu.make_async_copy(x_hbm.at[:, at], x_ref.at[:, at], in_sem.at[j])

    c_loads = [
        pltpu.make_async_copy(c_hbm.at[pl.ds(n * 256, 256)], c_ref.at[pl.ds(n * 256, 256)], in_sem.at[8 + n])
        for n in range(4)
    ]
    small_loads = [
        pltpu.make_async_copy(a, b, in_sem.at[12 + n])
        for n, (a, b) in enumerate([
            (gain_hbm, gain_ref), (rprev_hbm, rprev_ref), (cprev_hbm, cprev_ref),
        ])
    ]
    x_load(0).start()
    for load in c_loads:
        load.start()
    for j in range(1, 4):
        x_load(j).start()
    greet(up)
    greet(down)
    for _, dev in group:
        greet(dev)
    for k in range(1, NCOL):
        greet({"col": cols4[k]})
    for load in c_loads:
        load.wait()
    for j in range(4, 8):
        x_load(j).start()
    for load in small_loads:
        load.start()

    def product(j):
        at = pl.ds(pl.multiple_of(block(j) * 128, 128), 128)
        x_load(j).wait()
        part[at, :] = lax.dot_general(
            x_ref[:, at], c_ref[...], (((0,), (0,)), ((), ())),
            preferred_element_type=F32,
        )

    def y_copy(e):
        rows_ = pl.ds(pl.multiple_of(e * ROWS + other * HALF, HALF), HALF)
        return remote(part.at[rows_, pl.ds(zf, WIDE - zf)], ybuf.at[e], ys.at[e], yr.at[e], pair)

    def y_send(j):
        p = block(j)
        y_copy(2 * p + upper(j)).start()
        y_copy(2 * p + 1 - upper(j)).start()

    def first(j, _):
        product(j)
        return 0

    def later(j, _):
        product(j)
        y_send(j)
        return 0

    def own(e, chunk):
        _, theirs, r0, nr, c0, w, _ = chunk
        h = other if theirs else c
        return part.at[pl.ds(pl.multiple_of(e * ROWS + h * HALF + r0, nr), nr), pl.ds(c0, w)]

    def dest(direction, distance):
        return lax.rem(d + (NZ - distance if direction else distance), NZ)

    def hop(direction, n, i, src):
        ch = direction * nch + n
        return remote(
            src, rbufs[n].at[direction, i], ssem.at[ch, i], rsem.at[ch, i],
            {"dp": dest(direction, 1)},
        )

    def begin(direction, n, i):
        hop(direction, n, i, own(dest(direction, 8 - i), chunks[n])).start()

    def forward(direction, n, i):
        slot = rbufs[n].at[direction, i - 1]
        hop(direction, n, i - 1, slot).wait_recv()
        slot[...] += own(dest(direction, 8 - i), chunks[n])[...]
        hop(direction, n, i, slot).start()

    def y_add(e):
        y_copy(e).wait_recv()
        rows_ = pl.ds(pl.multiple_of(e * ROWS + c * HALF, HALF), HALF)
        part[rows_, pl.ds(zf, WIDE - zf)] += ybuf[e]

    zn = range(len(zc))
    yn = range(len(zc), nch)

    def start0(which_n):
        for n in which_n:
            begin(chunks[n][6], n, 0)

    def start1(which_n):
        for n in which_n:
            begin(1 - chunks[n][6], n, 1)

    def second(which_n):
        for n in which_n:
            forward(chunks[n][6], n, 1)

    def z_step(i):
        for ahead in (1, 0):
            for n in zn:
                forward(chunks[n][6] ^ ahead, n, i)

    def y_step(i):
        for direction in (0, 1):
            y_add(dest(direction, 8 - i))
        for ahead in (1, 0):
            for n in yn:
                forward(chunks[n][6] ^ ahead, n, i)

    def fill(j, _):
        product(j)

        @pl.when(j == 0)
        def _():
            pl.semaphore_wait(barrier, 2 + (N8 - 1) + (NCOL - 1))
            start0(zn)

        y_send(j)

        @pl.when(j == 1)
        def _():
            start1(zn)

        @pl.when(j == 6)
        def _():
            second(zn)

        return 0

    lax.fori_loop(0, 8, fill, 0)
    for load in small_loads:
        load.wait()
    y_add(dest(0, 8))
    start0(yn)
    z_step(2)
    for direction in (0, 1):
        y_add(dest(direction, 7))
    start1(yn)
    second(yn)

    def steps(i, _):
        z_step(i)
        y_step(i - 1)
        return 0

    lax.fori_loop(3, 8, steps, 0)

    def collect(n):
        for direction in (0, 1):
            hop(direction, n, 7, rbufs[n].at[direction, 7]).wait_recv()
        return own(d, chunks[n])[...] + rbufs[n][0, 7] + rbufs[n][1, 7]

    for n in zn:
        _, theirs, r0, nr, c0, w, _ = chunks[n]
        if theirs:
            zx_src[:, pl.ds(c0, w)] = collect(n)
    zx = remote(zx_src, zx_dst, zxs, zxr, pair)
    zx.start()
    y_step(7)
    y_add(d)

    lane = lax.broadcasted_iota(jnp.int32, (HALF, WIDE), 1)
    sub = lax.broadcasted_iota(jnp.int32, (HALF, WIDE), 0)
    gain = jnp.sum(
        jnp.where(lane == sub + d * ROWS + c * HALF, gain_ref[...], 0.0), axis=1, keepdims=True
    )
    mine = pl.ds(pl.multiple_of(c * HALF, HALF), HALF)
    for n in zn:
        _, theirs, r0, nr, c0, w, _ = chunks[n]
        if not theirs:
            gfull[mine, pl.ds(c0, w)] = collect(n)
    zx.wait_recv()
    gfull[mine, pl.ds(0, zf)] += zx_dst[...]
    for n in yn:
        _, theirs, r0, nr, c0, w, _ = chunks[n]
        gfull[pl.ds(pl.multiple_of(c * HALF + r0, nr), nr), pl.ds(c0, w)] = collect(n)
    g = gfull[mine, :] * gain
    gfull[mine, :] = g
    g_copy = remote(gfull.at[mine], gfull.at[mine], gs, gr, pair)

    lane1 = lax.broadcasted_iota(jnp.int32, (HALF, 128), 1)
    sub1 = lax.broadcasted_iota(jnp.int32, (HALF, 128), 0)
    diag = lane1 == sub1 + c * HALF
    sq = g * g
    rsum = jnp.sum(sq, axis=1, keepdims=True)
    rr[col] = jnp.sum(jnp.where(diag, rsum, 0.0), axis=0, keepdims=True)
    rcopies = []
    for k in range(1, NCOL):
        to = cols4[k]
        cp = remote(rr.at[col], rr.at[col], rs.at[k], rrs.at[col], {"col": to})
        cp.start()
        rcopies.append(cp)
    g_copy.start()
    asum = jnp.sum(sq, axis=0, keepdims=True)
    for e in range(N8):
        ab_src[e, :, pl.ds(0, 128)] = asum[:, e * 128:(e + 1) * 128]
    for k in range(1, NCOL):
        frm = cols4[k]
        remote(rr.at[frm], rr.at[frm], rs.at[k], rrs.at[frm], {"col": frm}).wait_recv()
    total = rr[0] + rr[1] + rr[2] + rr[3]
    lane_r = lax.broadcasted_iota(jnp.int32, (1, 128), 1)
    in_half = (lane_r >= c * HALF) & (lane_r < c * HALF + HALF)
    rprev = jnp.concatenate([rprev_ref[...], rprev_ref[...]], axis=1)
    rmom = DECAY * rprev + (1.0 - DECAY) * (total / F + EPS)
    rmom = jnp.where(in_half, rmom, 0.0)
    rcol = jnp.sum(jnp.where(diag, rmom, 0.0), axis=1, keepdims=True)
    bsum = jnp.sum(sq * (1.0 / rcol), axis=0, keepdims=True)
    for e in range(N8):
        ab_src[e, :, pl.ds(128, 128)] = bsum[:, e * 128:(e + 1) * 128]

    acopies = []
    for k, (e, dev) in enumerate(group):
        cp = remote(ab_src.at[e], ab.at[me8], abs_.at[k], abr.at[me8], dev)
        cp.start()
        acopies.append(cp)
    rx_src[...] = rmom
    rx = remote(rx_src, rx_dst, rxs, rxr, pair)
    rx.start()
    ab[me8] = ab_src[me8]
    for k, (e, dev) in enumerate(group):
        remote(ab_src.at[e], ab.at[e], abs_.at[k], abr.at[e], dev).wait_recv()
    acc = ab[0]
    for e in range(1, N8):
        acc = acc + ab[e]

    zab[d] = acc
    zcopies = []
    order = [8] + [k for m in range(7, 0, -1) for k in (m, 16 - m)]
    for k in order:
        to = lax.rem(d + k, NZ)
        cp = remote(zab.at[d], zab.at[d], zs.at[k], zr.at[d], {"dp": to})
        cp.start()
        zcopies.append(cp)
    cprev = cprev_ref[:, pl.ds(pl.multiple_of(me8 * 128, 128), 128)]
    for k in reversed(order):
        frm = lax.rem(d + k, NZ)
        remote(zab.at[frm], zab.at[frm], zs.at[k], zr.at[frm], {"dp": frm}).wait_recv()
    acc = zab[0]
    for e in range(1, NZ):
        acc = acc + zab[e]
    cmom = DECAY * cprev + (1.0 - DECAY) * (acc[:, 0:128] / D + EPS)
    fin[me32, :, pl.ds(0, 128)] = cmom
    fin[me32, :, pl.ds(128, 128)] = acc[:, 128:256] / cmom

    fcopies = []
    for k, (_, dev) in enumerate(plane):
        cp = remote(fin.at[me32], fin.at[me32], fs.at[k], fr.at[me32], dev)
        cp.start()
        fcopies.append(cp)

    rx.wait_recv()
    rfull = rmom + rx_dst[...]
    rmom_ref[...] = rfull[:, 0:ROWS]
    lane2 = lax.broadcasted_iota(jnp.int32, (ROWS, 128), 1)
    sub2 = lax.broadcasted_iota(jnp.int32, (ROWS, 128), 0)
    rscale = lax.rsqrt(jnp.sum(jnp.where(lane2 == sub2, rfull, 0.0), axis=1, keepdims=True))
    g_copy.wait_recv()

    for n in range(nch):
        for direction in (0, 1):
            lo = 0 if direction == chunks[n][6] else 1

            def drain(i, _, direction=direction, n=n):
                hop(direction, n, i, rbufs[n].at[direction, i]).wait_send()
                return 0

            lax.fori_loop(lo, 8, drain, 0)

    def drain_y(e, _):
        y_copy(e).wait_send()
        return 0

    lax.fori_loop(0, NZ, drain_y, 0)
    zx.wait_send()
    g_copy.wait_send()
    rx.wait_send()
    for cp in rcopies + acopies + zcopies:
        cp.wait_send()

    for k, (e, dev) in enumerate(plane):
        remote(fin.at[e], fin.at[e], fs.at[k], fr.at[e], dev).wait_recv()
    tot = fin[0, :, pl.ds(128, 128)]
    for e in range(1, N32):
        tot = tot + fin[e, :, pl.ds(128, 128)]
    ratio = jnp.sum(tot, axis=1, keepdims=True) / (D * F)
    inverse = 1.0 / jnp.maximum(1.0, jnp.sqrt(ratio) / CLIP)
    rows_scale = rscale * inverse
    for e in range(N8):
        at = pl.ds(e * 128, 128)
        cm = fin[col * N8 + e, :, pl.ds(0, 128)]
        cmom_ref[:, at] = cm
        upd_ref[:, at] = gfull[:, at] * rows_scale * lax.rsqrt(cm)
    for cp in fcopies:
        cp.wait_send()


def call(cfg, cid, name, tokens, cotangent, norm_gain, row_prev, col_prev):
    zc, yc = make_chunks(cfg)
    chunks = zc + yc
    nch = len(chunks)
    zf = cfg["zf"]
    vmem = pl.BlockSpec(memory_space=pltpu.VMEM)
    hbm = pl.BlockSpec(memory_space=pltpu.HBM)
    dma = pltpu.SemaphoreType.DMA
    bf = jnp.bfloat16
    return pl.pallas_call(
        functools.partial(kernel, cfg),
        out_shape=(
            jax.ShapeDtypeStruct((ROWS, WIDE), F32),
            jax.ShapeDtypeStruct((1, ROWS), F32),
            jax.ShapeDtypeStruct((1, WIDE), F32),
        ),
        in_specs=[hbm] * 5,
        out_specs=(vmem, vmem, vmem),
        scratch_shapes=[
            pltpu.VMEM((1024, 1024), bf),
            pltpu.VMEM((1024, 1024), bf),
            pltpu.VMEM((1, 1024), F32),
            pltpu.VMEM((1, ROWS), F32),
            pltpu.VMEM((1, WIDE), F32),
            pltpu.VMEM((1024, WIDE), F32),
        ] + [pltpu.VMEM((2, 8, ch[3], ch[5]), F32) for ch in chunks] + [
            pltpu.VMEM((NZ, HALF, WIDE - zf), F32),
            pltpu.VMEM((HALF, zf), F32),
            pltpu.VMEM((HALF, zf), F32),
            pltpu.VMEM((ROWS, WIDE), F32),
            pltpu.VMEM((NCOL, 1, 128), F32),
            pltpu.VMEM((1, 128), F32),
            pltpu.VMEM((1, 128), F32),
            pltpu.VMEM((N8, 1, 256), F32),
            pltpu.VMEM((N8, 1, 256), F32),
            pltpu.VMEM((NZ, 1, 256), F32),
            pltpu.VMEM((N32, 1, 256), F32),
            dma((15,)),
            dma((2 * nch, 8)), dma((2 * nch, 8)),
            dma((NZ,)), dma((NZ,)),
            dma, dma, dma, dma,
            dma((NCOL,)), dma((NCOL,)),
            dma, dma,
            dma((N8,)), dma((N8,)),
            dma((NZ,)), dma((NZ,)),
            dma((N32,)), dma((N32,)),
        ],
        compiler_params=pltpu.CompilerParams(
            collective_id=cid, has_side_effects=True, vmem_limit_bytes=56 << 20
        ),
        name=name,
    )(tokens, cotangent, norm_gain[None, :], row_prev, col_prev[None, :])


def write(u, r, c, uo, ro, co, sem):
    copies = [
        pltpu.make_async_copy(a, b, sem.at[n]) for n, (a, b) in enumerate([(u, uo), (r, ro), (c, co)])
    ]
    for cp in copies:
        cp.start()
    for cp in copies:
        cp.wait()


def body(tokens, cotangent, norm_gain, row_prev, col_prev):
    vmem = pl.BlockSpec(memory_space=pltpu.VMEM)
    hbm = pl.BlockSpec(memory_space=pl.ANY)
    u, r, c = call(CFG, 0, "adafactor", tokens, cotangent, norm_gain, row_prev, col_prev)
    u, r, c = pl.pallas_call(
        write,
        out_shape=tuple(jax.ShapeDtypeStruct(a.shape, F32) for a in (u, r, c)),
        in_specs=[hbm] * 3,
        out_specs=(hbm,) * 3,
        scratch_shapes=[pltpu.SemaphoreType.DMA((3,))],
        compiler_params=pltpu.CompilerParams(vmem_limit_bytes=60 << 20),
        name="write",
    )(u, r, c)
    return u[None], r, c[0]


CFG = {"zf": 384, "zs": 1, "ys": 1}


def solution(mesh):
    return jax.shard_map(
        body,
        mesh=mesh,
        in_specs=(
            P(("cuts", "dp"), "row"),
            P(("cuts", "dp"), "col"),
            P("row"),
            P("row", "dp"),
            P("col"),
        ),
        out_specs=(P("row", "dp", "col"), P("row", "dp"), P("col")),
        check_vma=False,
    )
```

```python
import functools

import jax
import jax.numpy as jnp
from jax import lax
from jax.experimental import pallas as pl
from jax.experimental.pallas import tpu as pltpu
from jax.sharding import PartitionSpec as P

MESH = pl.DeviceIdType.MESH
F32 = jnp.float32

D = 4096
F = 4096
DECAY = 0.975
EPS = 1e-30
CLIP = 1.0

NZ, NROW, NCOL, NCUT = 16, 4, 4, 2
N8 = NROW * NCUT
N32 = NCOL * N8
ROWS = 64
HALF = 32
WIDE = 1024


def make_chunks(cfg):
    zf, zs, yk = cfg["zf"], cfg["zs"], cfg["ys"]
    z, y = [], []
    for theirs in (1, 0):
        for q in range(zs):
            z.append((0, theirs, 0, HALF, q * (zf // zs), zf // zs, (1 - theirs + q) % 2))
    yw = (WIDE - zf) // yk
    for q in range(yk):
        for r in range(2):
            y.append((1, 0, r * 16, 16, zf + q * yw, yw, (r + q) % 2))
    return z, y


def kernel(cfg, *refs):
    zc, yc = make_chunks(cfg)
    chunks = zc + yc
    nch = len(chunks)
    zf = cfg["zf"]
    (x_hbm, c_hbm, gain_hbm, rprev_hbm, cprev_hbm, upd_hbm, rmom_hbm, cmom_hbm,
     upd_ref, rmom_ref, cmom_ref, out_sem,
     x_ref, c_ref, gain_ref, rprev_ref, cprev_ref, part) = refs[:18]
    rbufs = refs[18:18 + nch]
    (ybuf, zx_src, zx_dst, gfull, rr, rx_src, rx_dst, ab_src, ab, zab, fin,
     in_sem, ssem, rsem, ys, yr, zxs, zxr, gs, gr, rs, rrs, rxs, rxr, abs_, abr, zs, zr, fs, fr,
     ) = refs[18 + nch:]
    d = lax.axis_index("dp")
    c = lax.axis_index("cuts")
    row = lax.axis_index("row")
    col = lax.axis_index("col")
    other = 1 - c
    me8 = row * NCUT + c
    me32 = col * N8 + me8
    up = {"dp": lax.rem(d + 1, NZ)}
    down = {"dp": lax.rem(d + NZ - 1, NZ)}
    pair = {"cuts": other}

    rows4 = [lax.rem(row + k, NROW) for k in range(NROW)]
    cols4 = [lax.rem(col + k, NCOL) for k in range(NCOL)]
    cuts2 = [c, other]

    group = [
        (rows4[a] * NCUT + cuts2[b], {"row": rows4[a], "cuts": cuts2[b]})
        for a in range(NROW) for b in range(NCUT) if a or b
    ]
    plane = [
        (cols4[k] * N8 + rows4[a] * NCUT + cuts2[b], {"col": cols4[k], "row": rows4[a], "cuts": cuts2[b]})
        for k in (2, 1, 3, 0) for a in (2, 1, 3, 0) for b in (1, 0) if k or a or b
    ]

    def remote(src, dst, s, r, dev):
        return pltpu.make_async_remote_copy(
            src_ref=src, dst_ref=dst, send_sem=s, recv_sem=r,
            device_id=dev, device_id_type=MESH,
        )

    barrier = pltpu.get_barrier_semaphore()

    def greet(dev):
        pl.semaphore_signal(barrier, inc=1, device_id=dev, device_id_type=MESH)

    def upper(j):
        return lax.rem(j + d, 2)

    def block(j):
        return lax.rem(d // 2 + 12 + (1 - 2 * upper(j)) * ((j + 1) // 2), 8)

    def x_load(j):
        at = pl.ds(pl.multiple_of(block(j) * 128, 128), 128)
        return pltpu.make_async_copy(x_hbm.at[:, at], x_ref.at[:, at], in_sem.at[j])

    c_loads = [
        pltpu.make_async_copy(c_hbm.at[pl.ds(n * 256, 256)], c_ref.at[pl.ds(n * 256, 256)], in_sem.at[8 + n])
        for n in range(4)
    ]
    small_loads = [
        pltpu.make_async_copy(a, b, in_sem.at[12 + n])
        for n, (a, b) in enumerate([
            (gain_hbm, gain_ref), (rprev_hbm, rprev_ref), (cprev_hbm, cprev_ref),
        ])
    ]
    x_load(0).start()
    for load in c_loads:
        load.start()
    for j in range(1, 4):
        x_load(j).start()
    greet(up)
    greet(down)
    for _, dev in group:
        greet(dev)
    for k in range(1, NCOL):
        greet({"col": cols4[k]})
    for load in c_loads:
        load.wait()
    for j in range(4, 8):
        x_load(j).start()
    for load in small_loads:
        load.start()

    def product(j):
        at = pl.ds(pl.multiple_of(block(j) * 128, 128), 128)
        x_load(j).wait()
        part[at, :] = lax.dot_general(
            x_ref[:, at], c_ref[...], (((0,), (0,)), ((), ())),
            preferred_element_type=F32,
        )

    def y_copy(e):
        rows_ = pl.ds(pl.multiple_of(e * ROWS + other * HALF, HALF), HALF)
        return remote(part.at[rows_, pl.ds(zf, WIDE - zf)], ybuf.at[e], ys.at[e], yr.at[e], pair)

    def y_send(j):
        p = block(j)
        y_copy(2 * p + upper(j)).start()
        y_copy(2 * p + 1 - upper(j)).start()

    def first(j, _):
        product(j)
        return 0

    def later(j, _):
        product(j)
        y_send(j)
        return 0

    def own(e, chunk):
        _, theirs, r0, nr, c0, w, _ = chunk
        h = other if theirs else c
        return part.at[pl.ds(pl.multiple_of(e * ROWS + h * HALF + r0, nr), nr), pl.ds(c0, w)]

    def dest(direction, distance):
        return lax.rem(d + (NZ - distance if direction else distance), NZ)

    def hop(direction, n, i, src):
        ch = direction * nch + n
        return remote(
            src, rbufs[n].at[direction, i], ssem.at[ch, i], rsem.at[ch, i],
            {"dp": dest(direction, 1)},
        )

    def begin(direction, n, i):
        hop(direction, n, i, own(dest(direction, 8 - i), chunks[n])).start()

    def forward(direction, n, i):
        slot = rbufs[n].at[direction, i - 1]
        hop(direction, n, i - 1, slot).wait_recv()
        slot[...] += own(dest(direction, 8 - i), chunks[n])[...]
        hop(direction, n, i, slot).start()

    def y_add(e):
        y_copy(e).wait_recv()
        rows_ = pl.ds(pl.multiple_of(e * ROWS + c * HALF, HALF), HALF)
        part[rows_, pl.ds(zf, WIDE - zf)] += ybuf[e]

    zn = range(len(zc))
    yn = range(len(zc), nch)

    def start0(which_n):
        for n in which_n:
            begin(chunks[n][6], n, 0)

    def start1(which_n):
        for n in which_n:
            begin(1 - chunks[n][6], n, 1)

    def second(which_n):
        for n in which_n:
            forward(chunks[n][6], n, 1)

    def z_step(i):
        for ahead in (1, 0):
            for n in zn:
                forward(chunks[n][6] ^ ahead, n, i)

    def y_step(i):
        for direction in (0, 1):
            y_add(dest(direction, 8 - i))
        for ahead in (1, 0):
            for n in yn:
                forward(chunks[n][6] ^ ahead, n, i)

    def fill(j, _):
        product(j)

        @pl.when(j == 0)
        def _():
            pl.semaphore_wait(barrier, 2 + (N8 - 1) + (NCOL - 1))
            start0(zn)

        y_send(j)

        @pl.when(j == 1)
        def _():
            start1(zn)

        @pl.when(j == 6)
        def _():
            second(zn)

        return 0

    lax.fori_loop(0, 8, fill, 0)
    for load in small_loads:
        load.wait()
    y_add(dest(0, 8))
    start0(yn)
    z_step(2)
    for direction in (0, 1):
        y_add(dest(direction, 7))
    start1(yn)
    second(yn)

    def steps(i, _):
        z_step(i)
        y_step(i - 1)
        return 0

    lax.fori_loop(3, 8, steps, 0)

    def collect(n):
        for direction in (0, 1):
            hop(direction, n, 7, rbufs[n].at[direction, 7]).wait_recv()
        return own(d, chunks[n])[...] + rbufs[n][0, 7] + rbufs[n][1, 7]

    for n in zn:
        _, theirs, r0, nr, c0, w, _ = chunks[n]
        if theirs:
            zx_src[:, pl.ds(c0, w)] = collect(n)
    zx = remote(zx_src, zx_dst, zxs, zxr, pair)
    zx.start()
    y_step(7)
    y_add(d)

    lane = lax.broadcasted_iota(jnp.int32, (HALF, WIDE), 1)
    sub = lax.broadcasted_iota(jnp.int32, (HALF, WIDE), 0)
    gain = jnp.sum(
        jnp.where(lane == sub + d * ROWS + c * HALF, gain_ref[...], 0.0), axis=1, keepdims=True
    )
    mine = pl.ds(pl.multiple_of(c * HALF, HALF), HALF)
    for n in zn:
        _, theirs, r0, nr, c0, w, _ = chunks[n]
        if not theirs:
            gfull[mine, pl.ds(c0, w)] = collect(n)
    zx.wait_recv()
    gfull[mine, pl.ds(0, zf)] += zx_dst[...]
    for n in yn:
        _, theirs, r0, nr, c0, w, _ = chunks[n]
        gfull[pl.ds(pl.multiple_of(c * HALF + r0, nr), nr), pl.ds(c0, w)] = collect(n)
    g = gfull[mine, :] * gain
    gfull[mine, :] = g
    g_copy = remote(gfull.at[mine], gfull.at[mine], gs, gr, pair)

    lane1 = lax.broadcasted_iota(jnp.int32, (HALF, 128), 1)
    sub1 = lax.broadcasted_iota(jnp.int32, (HALF, 128), 0)
    diag = lane1 == sub1 + c * HALF
    sq = g * g
    rsum = jnp.sum(sq, axis=1, keepdims=True)
    rr[col] = jnp.sum(jnp.where(diag, rsum, 0.0), axis=0, keepdims=True)
    rcopies = []
    for k in range(1, NCOL):
        to = cols4[k]
        cp = remote(rr.at[col], rr.at[col], rs.at[k], rrs.at[col], {"col": to})
        cp.start()
        rcopies.append(cp)
    g_copy.start()
    asum = jnp.sum(sq, axis=0, keepdims=True)
    for e in range(N8):
        ab_src[e, :, pl.ds(0, 128)] = asum[:, e * 128:(e + 1) * 128]
    for k in range(1, NCOL):
        frm = cols4[k]
        remote(rr.at[frm], rr.at[frm], rs.at[k], rrs.at[frm], {"col": frm}).wait_recv()
    total = rr[0] + rr[1] + rr[2] + rr[3]
    lane_r = lax.broadcasted_iota(jnp.int32, (1, 128), 1)
    in_half = (lane_r >= c * HALF) & (lane_r < c * HALF + HALF)
    rprev = jnp.concatenate([rprev_ref[...], rprev_ref[...]], axis=1)
    rmom = DECAY * rprev + (1.0 - DECAY) * (total / F + EPS)
    rmom = jnp.where(in_half, rmom, 0.0)
    rcol = jnp.sum(jnp.where(diag, rmom, 0.0), axis=1, keepdims=True)
    bsum = jnp.sum(sq * (1.0 / rcol), axis=0, keepdims=True)
    for e in range(N8):
        ab_src[e, :, pl.ds(128, 128)] = bsum[:, e * 128:(e + 1) * 128]

    acopies = []
    for k, (e, dev) in enumerate(group):
        cp = remote(ab_src.at[e], ab.at[me8], abs_.at[k], abr.at[me8], dev)
        cp.start()
        acopies.append(cp)
    rx_src[...] = rmom
    rx = remote(rx_src, rx_dst, rxs, rxr, pair)
    rx.start()
    ab[me8] = ab_src[me8]
    for k, (e, dev) in enumerate(group):
        remote(ab_src.at[e], ab.at[e], abs_.at[k], abr.at[e], dev).wait_recv()
    acc = ab[0]
    for e in range(1, N8):
        acc = acc + ab[e]

    zab[d] = acc
    zcopies = []
    order = [8] + [k for m in range(7, 0, -1) for k in (m, 16 - m)]
    for k in order:
        to = lax.rem(d + k, NZ)
        cp = remote(zab.at[d], zab.at[d], zs.at[k], zr.at[d], {"dp": to})
        cp.start()
        zcopies.append(cp)
    cprev = cprev_ref[:, pl.ds(pl.multiple_of(me8 * 128, 128), 128)]
    for k in reversed(order):
        frm = lax.rem(d + k, NZ)
        remote(zab.at[frm], zab.at[frm], zs.at[k], zr.at[frm], {"dp": frm}).wait_recv()
    acc = zab[0]
    for e in range(1, NZ):
        acc = acc + zab[e]
    cmom = DECAY * cprev + (1.0 - DECAY) * (acc[:, 0:128] / D + EPS)
    fin[me32, :, pl.ds(0, 128)] = cmom
    fin[me32, :, pl.ds(128, 128)] = acc[:, 128:256] / cmom

    fcopies = []
    for k, (_, dev) in enumerate(plane):
        cp = remote(fin.at[me32], fin.at[me32], fs.at[k], fr.at[me32], dev)
        cp.start()
        fcopies.append(cp)

    rx.wait_recv()
    rfull = rmom + rx_dst[...]
    rmom_ref[...] = rfull[:, 0:ROWS]
    outs = [pltpu.make_async_copy(rmom_ref, rmom_hbm, out_sem.at[N8])]
    outs[0].start()
    lane2 = lax.broadcasted_iota(jnp.int32, (ROWS, 128), 1)
    sub2 = lax.broadcasted_iota(jnp.int32, (ROWS, 128), 0)
    rscale = lax.rsqrt(jnp.sum(jnp.where(lane2 == sub2, rfull, 0.0), axis=1, keepdims=True))
    g_copy.wait_recv()

    for n in range(nch):
        for direction in (0, 1):
            lo = 0 if direction == chunks[n][6] else 1

            def drain(i, _, direction=direction, n=n):
                hop(direction, n, i, rbufs[n].at[direction, i]).wait_send()
                return 0

            lax.fori_loop(lo, 8, drain, 0)

    def drain_y(e, _):
        y_copy(e).wait_send()
        return 0

    lax.fori_loop(0, NZ, drain_y, 0)
    zx.wait_send()
    g_copy.wait_send()
    rx.wait_send()
    for cp in rcopies + acopies + zcopies:
        cp.wait_send()

    for k, (e, dev) in enumerate(plane):
        remote(fin.at[e], fin.at[e], fs.at[k], fr.at[e], dev).wait_recv()
    tot = fin[0, :, pl.ds(128, 128)]
    for e in range(1, N32):
        tot = tot + fin[e, :, pl.ds(128, 128)]
    ratio = jnp.sum(tot, axis=1, keepdims=True) / (D * F)
    inverse = 1.0 / jnp.maximum(1.0, jnp.sqrt(ratio) / CLIP)
    rows_scale = rscale * inverse
    for e in range(N8):
        at = pl.ds(e * 128, 128)
        cm = fin[col * N8 + e, :, pl.ds(0, 128)]
        cmom_ref[:, at] = cm
        upd_ref[:, at] = gfull[:, at] * rows_scale * lax.rsqrt(cm)
        outs.append(pltpu.make_async_copy(upd_ref.at[:, at], upd_hbm.at[:, at], out_sem.at[e]))
        outs[-1].start()
    outs.append(pltpu.make_async_copy(cmom_ref, cmom_hbm, out_sem.at[N8 + 1]))
    outs[-1].start()
    for cp in fcopies:
        cp.wait_send()
    for cp in outs:
        cp.wait()


def call(cfg, cid, name, tokens, cotangent, norm_gain, row_prev, col_prev):
    zc, yc = make_chunks(cfg)
    chunks = zc + yc
    nch = len(chunks)
    zf = cfg["zf"]
    hbm = pl.BlockSpec(memory_space=pl.ANY)
    dma = pltpu.SemaphoreType.DMA
    bf = jnp.bfloat16
    return pl.pallas_call(
        functools.partial(kernel, cfg),
        out_shape=(
            jax.ShapeDtypeStruct((ROWS, WIDE), F32),
            jax.ShapeDtypeStruct((1, ROWS), F32),
            jax.ShapeDtypeStruct((1, WIDE), F32),
        ),
        in_specs=[hbm] * 5,
        out_specs=(hbm, hbm, hbm),
        scratch_shapes=[
            pltpu.VMEM((ROWS, WIDE), F32),
            pltpu.VMEM((1, ROWS), F32),
            pltpu.VMEM((1, WIDE), F32),
            dma((N8 + 2,)),
            pltpu.VMEM((1024, 1024), bf),
            pltpu.VMEM((1024, 1024), bf),
            pltpu.VMEM((1, 1024), F32),
            pltpu.VMEM((1, ROWS), F32),
            pltpu.VMEM((1, WIDE), F32),
            pltpu.VMEM((1024, WIDE), F32),
        ] + [pltpu.VMEM((2, 8, ch[3], ch[5]), F32) for ch in chunks] + [
            pltpu.VMEM((NZ, HALF, WIDE - zf), F32),
            pltpu.VMEM((HALF, zf), F32),
            pltpu.VMEM((HALF, zf), F32),
            pltpu.VMEM((ROWS, WIDE), F32),
            pltpu.VMEM((NCOL, 1, 128), F32),
            pltpu.VMEM((1, 128), F32),
            pltpu.VMEM((1, 128), F32),
            pltpu.VMEM((N8, 1, 256), F32),
            pltpu.VMEM((N8, 1, 256), F32),
            pltpu.VMEM((NZ, 1, 256), F32),
            pltpu.VMEM((N32, 1, 256), F32),
            dma((15,)),
            dma((2 * nch, 8)), dma((2 * nch, 8)),
            dma((NZ,)), dma((NZ,)),
            dma, dma, dma, dma,
            dma((NCOL,)), dma((NCOL,)),
            dma, dma,
            dma((N8,)), dma((N8,)),
            dma((NZ,)), dma((NZ,)),
            dma((N32,)), dma((N32,)),
        ],
        compiler_params=pltpu.CompilerParams(
            collective_id=cid, has_side_effects=True, vmem_limit_bytes=56 << 20
        ),
        name=name,
    )(tokens, cotangent, norm_gain[None, :], row_prev, col_prev[None, :])


def write(u, r, c, uo, ro, co, uv, rv, cv, isem, osem):
    pieces = 4
    rows_ = [pl.ds(n * (ROWS // pieces), ROWS // pieces) for n in range(pieces)]
    pairs = [(u.at[at], uv.at[at], uo.at[at]) for at in rows_] + [(r, rv, ro), (c, cv, co)]
    ins = [pltpu.make_async_copy(a, b, isem.at[n]) for n, (a, b, _) in enumerate(pairs)]
    outs = [pltpu.make_async_copy(b, o, osem.at[n]) for n, (_, b, o) in enumerate(pairs)]
    for cp in ins:
        cp.start()
    for a, b in zip(ins, outs):
        a.wait()
        b.start()
    for cp in outs:
        cp.wait()


def body(tokens, cotangent, norm_gain, row_prev, col_prev):
    hbm = pl.BlockSpec(memory_space=pl.ANY)
    u, r, c = call(CFG, 0, "adafactor", tokens, cotangent, norm_gain, row_prev, col_prev)
    u, r, c = pl.pallas_call(
        write,
        out_shape=tuple(jax.ShapeDtypeStruct(a.shape, F32) for a in (u, r, c)),
        in_specs=[hbm] * 3,
        out_specs=(hbm,) * 3,
        scratch_shapes=[
            pltpu.VMEM((ROWS, WIDE), F32),
            pltpu.VMEM((1, ROWS), F32),
            pltpu.VMEM((1, WIDE), F32),
            pltpu.SemaphoreType.DMA((6,)),
            pltpu.SemaphoreType.DMA((6,)),
        ],
        compiler_params=pltpu.CompilerParams(vmem_limit_bytes=60 << 20),
        name="write",
    )(u, r, c)
    return u[None], r, c[0]


CFG = {"zf": 384, "zs": 1, "ys": 1}


def solution(mesh):
    return jax.shard_map(
        body,
        mesh=mesh,
        in_specs=(
            P(("cuts", "dp"), "row"),
            P(("cuts", "dp"), "col"),
            P("row"),
            P("row", "dp"),
            P("col"),
        ),
        out_specs=(P("row", "dp", "col"), P("row", "dp"), P("col")),
        check_vma=False,
    )
```

```python
import functools

import jax
import jax.numpy as jnp
from jax import lax
from jax.experimental import pallas as pl
from jax.experimental.pallas import tpu as pltpu
from jax.sharding import PartitionSpec as P

MESH = pl.DeviceIdType.MESH
F32 = jnp.float32

D = 4096
F = 4096
DECAY = 0.975
EPS = 1e-30
CLIP = 1.0

NZ, NROW, NCOL, NCUT = 16, 4, 4, 2
N8 = NROW * NCUT
N32 = NCOL * N8
ROWS = 64
HALF = 32
WIDE = 1024


def make_chunks(cfg):
    zf, zs, yk = cfg["zf"], cfg["zs"], cfg["ys"]
    z, y = [], []
    for theirs in (1, 0):
        for q in range(zs):
            z.append((0, theirs, 0, HALF, q * (zf // zs), zf // zs, (1 - theirs + q) % 2))
    yw = (WIDE - zf) // yk
    for q in range(yk):
        for r in range(2):
            y.append((1, 0, r * 16, 16, zf + q * yw, yw, (r + q) % 2))
    return z, y


def kernel(cfg, *refs):
    zc, yc = make_chunks(cfg)
    chunks = zc + yc
    nch = len(chunks)
    zf = cfg["zf"]
    (x_hbm, c_hbm, gain_hbm, rprev_hbm, cprev_hbm, upd_hbm, rmom_hbm, cmom_hbm,
     upd_ref, rmom_ref, cmom_ref, out_sem,
     x_ref, c_ref, gain_ref, rprev_ref, cprev_ref, part) = refs[:18]
    rbufs = refs[18:18 + nch]
    (ybuf, zx_src, zx_dst, gfull, rr, rx_src, rx_dst, ab_src, ab, zab, fin,
     in_sem, ssem, rsem, ys, yr, zxs, zxr, gs, gr, rs, rrs, rxs, rxr, abs_, abr, zs, zr, fs, fr,
     ) = refs[18 + nch:]
    d = lax.axis_index("dp")
    c = lax.axis_index("cuts")
    row = lax.axis_index("row")
    col = lax.axis_index("col")
    other = 1 - c
    me8 = row * NCUT + c
    me32 = col * N8 + me8
    up = {"dp": lax.rem(d + 1, NZ)}
    down = {"dp": lax.rem(d + NZ - 1, NZ)}
    pair = {"cuts": other}

    rows4 = [lax.rem(row + k, NROW) for k in range(NROW)]
    cols4 = [lax.rem(col + k, NCOL) for k in range(NCOL)]
    cuts2 = [c, other]

    group = [
        (rows4[a] * NCUT + cuts2[b], {"row": rows4[a], "cuts": cuts2[b]})
        for a in range(NROW) for b in range(NCUT) if a or b
    ]
    plane = [
        (cols4[k] * N8 + rows4[a] * NCUT + cuts2[b], {"col": cols4[k], "row": rows4[a], "cuts": cuts2[b]})
        for k in (2, 1, 3, 0) for a in (2, 1, 3, 0) for b in (1, 0) if k or a or b
    ]

    def remote(src, dst, s, r, dev):
        return pltpu.make_async_remote_copy(
            src_ref=src, dst_ref=dst, send_sem=s, recv_sem=r,
            device_id=dev, device_id_type=MESH,
        )

    barrier = pltpu.get_barrier_semaphore()

    def greet(dev):
        pl.semaphore_signal(barrier, inc=1, device_id=dev, device_id_type=MESH)

    def upper(j):
        return lax.rem(j + d, 2)

    def block(j):
        return lax.rem(d // 2 + 12 + (1 - 2 * upper(j)) * ((j + 1) // 2), 8)

    def x_load(j):
        at = pl.ds(pl.multiple_of(block(j) * 128, 128), 128)
        return pltpu.make_async_copy(x_hbm.at[:, at], x_ref.at[:, at], in_sem.at[j])

    c_loads = [
        pltpu.make_async_copy(c_hbm.at[pl.ds(n * 256, 256)], c_ref.at[pl.ds(n * 256, 256)], in_sem.at[8 + n])
        for n in range(4)
    ]
    small_loads = [
        pltpu.make_async_copy(a, b, in_sem.at[12 + n])
        for n, (a, b) in enumerate([
            (gain_hbm, gain_ref), (rprev_hbm, rprev_ref), (cprev_hbm, cprev_ref),
        ])
    ]
    x_load(0).start()
    for load in c_loads:
        load.start()
    for j in range(1, 4):
        x_load(j).start()
    greet(up)
    greet(down)
    for _, dev in group:
        greet(dev)
    for k in range(1, NCOL):
        greet({"col": cols4[k]})
    for load in c_loads:
        load.wait()
    for j in range(4, 8):
        x_load(j).start()
    for load in small_loads:
        load.start()

    def product(j):
        at = pl.ds(pl.multiple_of(block(j) * 128, 128), 128)
        x_load(j).wait()
        part[at, :] = lax.dot_general(
            x_ref[:, at], c_ref[...], (((0,), (0,)), ((), ())),
            preferred_element_type=F32,
        )

    def y_copy(e):
        rows_ = pl.ds(pl.multiple_of(e * ROWS + other * HALF, HALF), HALF)
        return remote(part.at[rows_, pl.ds(zf, WIDE - zf)], ybuf.at[e], ys.at[e], yr.at[e], pair)

    def y_send(j):
        p = block(j)
        y_copy(2 * p + upper(j)).start()
        y_copy(2 * p + 1 - upper(j)).start()

    def first(j, _):
        product(j)
        return 0

    def later(j, _):
        product(j)
        y_send(j)
        return 0

    def own(e, chunk):
        _, theirs, r0, nr, c0, w, _ = chunk
        h = other if theirs else c
        return part.at[pl.ds(pl.multiple_of(e * ROWS + h * HALF + r0, nr), nr), pl.ds(c0, w)]

    def dest(direction, distance):
        return lax.rem(d + (NZ - distance if direction else distance), NZ)

    def hop(direction, n, i, src):
        ch = direction * nch + n
        return remote(
            src, rbufs[n].at[direction, i], ssem.at[ch, i], rsem.at[ch, i],
            {"dp": dest(direction, 1)},
        )

    def begin(direction, n, i):
        hop(direction, n, i, own(dest(direction, 8 - i), chunks[n])).start()

    def forward(direction, n, i):
        slot = rbufs[n].at[direction, i - 1]
        hop(direction, n, i - 1, slot).wait_recv()
        slot[...] += own(dest(direction, 8 - i), chunks[n])[...]
        hop(direction, n, i, slot).start()

    def y_add(e):
        y_copy(e).wait_recv()
        rows_ = pl.ds(pl.multiple_of(e * ROWS + c * HALF, HALF), HALF)
        part[rows_, pl.ds(zf, WIDE - zf)] += ybuf[e]

    zn = range(len(zc))
    yn = range(len(zc), nch)

    def start0(which_n):
        for n in which_n:
            begin(chunks[n][6], n, 0)

    def start1(which_n):
        for n in which_n:
            begin(1 - chunks[n][6], n, 1)

    def second(which_n):
        for n in which_n:
            forward(chunks[n][6], n, 1)

    def z_step(i):
        for ahead in (1, 0):
            for n in zn:
                forward(chunks[n][6] ^ ahead, n, i)

    def y_step(i):
        for direction in (0, 1):
            y_add(dest(direction, 8 - i))
        for ahead in (1, 0):
            for n in yn:
                forward(chunks[n][6] ^ ahead, n, i)

    def fill(j, _):
        product(j)

        @pl.when(j == 0)
        def _():
            pl.semaphore_wait(barrier, 2 + (N8 - 1) + (NCOL - 1))
            start0(zn)

        y_send(j)

        @pl.when(j == 1)
        def _():
            start1(zn)

        @pl.when(j == 6)
        def _():
            second(zn)

        return 0

    lax.fori_loop(0, 8, fill, 0)
    for load in small_loads:
        load.wait()
    y_add(dest(0, 8))
    start0(yn)
    z_step(2)
    for direction in (0, 1):
        y_add(dest(direction, 7))
    start1(yn)
    second(yn)

    def steps(i, _):
        z_step(i)
        y_step(i - 1)
        return 0

    lax.fori_loop(3, 8, steps, 0)

    def collect(n):
        for direction in (0, 1):
            hop(direction, n, 7, rbufs[n].at[direction, 7]).wait_recv()
        return own(d, chunks[n])[...] + rbufs[n][0, 7] + rbufs[n][1, 7]

    for n in zn:
        _, theirs, r0, nr, c0, w, _ = chunks[n]
        if theirs:
            zx_src[:, pl.ds(c0, w)] = collect(n)
    zx = remote(zx_src, zx_dst, zxs, zxr, pair)
    zx.start()
    y_step(7)
    y_add(d)

    lane = lax.broadcasted_iota(jnp.int32, (HALF, WIDE), 1)
    sub = lax.broadcasted_iota(jnp.int32, (HALF, WIDE), 0)
    gain = jnp.sum(
        jnp.where(lane == sub + d * ROWS + c * HALF, gain_ref[...], 0.0), axis=1, keepdims=True
    )
    mine = pl.ds(pl.multiple_of(c * HALF, HALF), HALF)
    for n in zn:
        _, theirs, r0, nr, c0, w, _ = chunks[n]
        if not theirs:
            gfull[mine, pl.ds(c0, w)] = collect(n)
    zx.wait_recv()
    gfull[mine, pl.ds(0, zf)] += zx_dst[...]
    for n in yn:
        _, theirs, r0, nr, c0, w, _ = chunks[n]
        gfull[pl.ds(pl.multiple_of(c * HALF + r0, nr), nr), pl.ds(c0, w)] = collect(n)
    g = gfull[mine, :] * gain
    gfull[mine, :] = g
    g_copy = remote(gfull.at[mine], gfull.at[mine], gs, gr, pair)

    lane1 = lax.broadcasted_iota(jnp.int32, (HALF, 128), 1)
    sub1 = lax.broadcasted_iota(jnp.int32, (HALF, 128), 0)
    diag = lane1 == sub1 + c * HALF
    sq = g * g
    rsum = jnp.sum(sq, axis=1, keepdims=True)
    rr[col] = jnp.sum(jnp.where(diag, rsum, 0.0), axis=0, keepdims=True)
    rcopies = []
    for k in range(1, NCOL):
        to = cols4[k]
        cp = remote(rr.at[col], rr.at[col], rs.at[k], rrs.at[col], {"col": to})
        cp.start()
        rcopies.append(cp)
    g_copy.start()
    asum = jnp.sum(sq, axis=0, keepdims=True)
    for e in range(N8):
        ab_src[e, :, pl.ds(0, 128)] = asum[:, e * 128:(e + 1) * 128]
    for k in range(1, NCOL):
        frm = cols4[k]
        remote(rr.at[frm], rr.at[frm], rs.at[k], rrs.at[frm], {"col": frm}).wait_recv()
    total = rr[0] + rr[1] + rr[2] + rr[3]
    lane_r = lax.broadcasted_iota(jnp.int32, (1, 128), 1)
    in_half = (lane_r >= c * HALF) & (lane_r < c * HALF + HALF)
    rprev = jnp.concatenate([rprev_ref[...], rprev_ref[...]], axis=1)
    rmom = DECAY * rprev + (1.0 - DECAY) * (total / F + EPS)
    rmom = jnp.where(in_half, rmom, 0.0)
    rcol = jnp.sum(jnp.where(diag, rmom, 0.0), axis=1, keepdims=True)
    bsum = jnp.sum(sq * (1.0 / rcol), axis=0, keepdims=True)
    for e in range(N8):
        ab_src[e, :, pl.ds(128, 128)] = bsum[:, e * 128:(e + 1) * 128]

    acopies = []
    for k, (e, dev) in enumerate(group):
        cp = remote(ab_src.at[e], ab.at[me8], abs_.at[k], abr.at[me8], dev)
        cp.start()
        acopies.append(cp)
    rx_src[...] = rmom
    rx = remote(rx_src, rx_dst, rxs, rxr, pair)
    rx.start()
    ab[me8] = ab_src[me8]
    for k, (e, dev) in enumerate(group):
        remote(ab_src.at[e], ab.at[e], abs_.at[k], abr.at[e], dev).wait_recv()
    acc = ab[0]
    for e in range(1, N8):
        acc = acc + ab[e]

    zab[d] = acc
    zcopies = []
    order = [8] + [k for m in range(7, 0, -1) for k in (m, 16 - m)]
    for k in order:
        to = lax.rem(d + k, NZ)
        cp = remote(zab.at[d], zab.at[d], zs.at[k], zr.at[d], {"dp": to})
        cp.start()
        zcopies.append(cp)
    rx.wait_recv()
    rfull = rmom + rx_dst[...]
    rmom_ref[...] = rfull[:, 0:ROWS]
    outs = [pltpu.make_async_copy(rmom_ref, rmom_hbm, out_sem.at[N8])]
    outs[0].start()
    lane2 = lax.broadcasted_iota(jnp.int32, (ROWS, 128), 1)
    sub2 = lax.broadcasted_iota(jnp.int32, (ROWS, 128), 0)
    rscale = lax.rsqrt(jnp.sum(jnp.where(lane2 == sub2, rfull, 0.0), axis=1, keepdims=True))
    g_copy.wait_recv()
    upd_ref[...] = gfull[...] * rscale

    for n in range(nch):
        for direction in (0, 1):
            lo = 0 if direction == chunks[n][6] else 1

            def drain(i, _, direction=direction, n=n):
                hop(direction, n, i, rbufs[n].at[direction, i]).wait_send()
                return 0

            lax.fori_loop(lo, 8, drain, 0)

    def drain_y(e, _):
        y_copy(e).wait_send()
        return 0

    lax.fori_loop(0, NZ, drain_y, 0)
    zx.wait_send()
    g_copy.wait_send()
    rx.wait_send()
    for cp in rcopies + acopies:
        cp.wait_send()

    cprev = cprev_ref[:, pl.ds(pl.multiple_of(me8 * 128, 128), 128)]
    for k in reversed(order):
        frm = lax.rem(d + k, NZ)
        remote(zab.at[frm], zab.at[frm], zs.at[k], zr.at[frm], {"dp": frm}).wait_recv()
    acc = zab[0]
    for e in range(1, NZ):
        acc = acc + zab[e]
    cmom = DECAY * cprev + (1.0 - DECAY) * (acc[:, 0:128] / D + EPS)
    fin[me32, :, pl.ds(0, 128)] = cmom
    fin[me32, :, pl.ds(128, 128)] = acc[:, 128:256] / cmom

    fcopies = []
    for k, (_, dev) in enumerate(plane):
        cp = remote(fin.at[me32], fin.at[me32], fs.at[k], fr.at[me32], dev)
        cp.start()
        fcopies.append(cp)

    for k, (e, dev) in enumerate(plane):
        remote(fin.at[e], fin.at[e], fs.at[k], fr.at[e], dev).wait_recv()
    tot = fin[0, :, pl.ds(128, 128)]
    for e in range(1, N32):
        tot = tot + fin[e, :, pl.ds(128, 128)]
    ratio = jnp.sum(tot, axis=1, keepdims=True) / (D * F)
    inverse = 1.0 / jnp.maximum(1.0, jnp.sqrt(ratio) / CLIP)
    for e in range(N8):
        at = pl.ds(e * 128, 128)
        cm = fin[col * N8 + e, :, pl.ds(0, 128)]
        cmom_ref[:, at] = cm
        upd_ref[:, at] = upd_ref[:, at] * (lax.rsqrt(cm) * inverse)
        outs.append(pltpu.make_async_copy(upd_ref.at[:, at], upd_hbm.at[:, at], out_sem.at[e]))
        outs[-1].start()
    outs.append(pltpu.make_async_copy(cmom_ref, cmom_hbm, out_sem.at[N8 + 1]))
    outs[-1].start()
    for cp in zcopies + fcopies:
        cp.wait_send()
    for cp in outs:
        cp.wait()


def call(cfg, cid, name, tokens, cotangent, norm_gain, row_prev, col_prev):
    zc, yc = make_chunks(cfg)
    chunks = zc + yc
    nch = len(chunks)
    zf = cfg["zf"]
    hbm = pl.BlockSpec(memory_space=pl.ANY)
    dma = pltpu.SemaphoreType.DMA
    bf = jnp.bfloat16
    return pl.pallas_call(
        functools.partial(kernel, cfg),
        out_shape=(
            jax.ShapeDtypeStruct((ROWS, WIDE), F32),
            jax.ShapeDtypeStruct((1, ROWS), F32),
            jax.ShapeDtypeStruct((1, WIDE), F32),
        ),
        in_specs=[hbm] * 5,
        out_specs=(hbm, hbm, hbm),
        scratch_shapes=[
            pltpu.VMEM((ROWS, WIDE), F32),
            pltpu.VMEM((1, ROWS), F32),
            pltpu.VMEM((1, WIDE), F32),
            dma((N8 + 2,)),
            pltpu.VMEM((1024, 1024), bf),
            pltpu.VMEM((1024, 1024), bf),
            pltpu.VMEM((1, 1024), F32),
            pltpu.VMEM((1, ROWS), F32),
            pltpu.VMEM((1, WIDE), F32),
            pltpu.VMEM((1024, WIDE), F32),
        ] + [pltpu.VMEM((2, 8, ch[3], ch[5]), F32) for ch in chunks] + [
            pltpu.VMEM((NZ, HALF, WIDE - zf), F32),
            pltpu.VMEM((HALF, zf), F32),
            pltpu.VMEM((HALF, zf), F32),
            pltpu.VMEM((ROWS, WIDE), F32),
            pltpu.VMEM((NCOL, 1, 128), F32),
            pltpu.VMEM((1, 128), F32),
            pltpu.VMEM((1, 128), F32),
            pltpu.VMEM((N8, 1, 256), F32),
            pltpu.VMEM((N8, 1, 256), F32),
            pltpu.VMEM((NZ, 1, 256), F32),
            pltpu.VMEM((N32, 1, 256), F32),
            dma((15,)),
            dma((2 * nch, 8)), dma((2 * nch, 8)),
            dma((NZ,)), dma((NZ,)),
            dma, dma, dma, dma,
            dma((NCOL,)), dma((NCOL,)),
            dma, dma,
            dma((N8,)), dma((N8,)),
            dma((NZ,)), dma((NZ,)),
            dma((N32,)), dma((N32,)),
        ],
        compiler_params=pltpu.CompilerParams(
            collective_id=cid, has_side_effects=True, vmem_limit_bytes=56 << 20
        ),
        name=name,
    )(tokens, cotangent, norm_gain[None, :], row_prev, col_prev[None, :])


def write(u, r, c, uo, ro, co, uv, rv, cv, isem, osem):
    pieces = 4
    rows_ = [pl.ds(n * (ROWS // pieces), ROWS // pieces) for n in range(pieces)]
    pairs = [(u.at[at], uv.at[at], uo.at[at]) for at in rows_] + [(r, rv, ro), (c, cv, co)]
    ins = [pltpu.make_async_copy(a, b, isem.at[n]) for n, (a, b, _) in enumerate(pairs)]
    outs = [pltpu.make_async_copy(b, o, osem.at[n]) for n, (_, b, o) in enumerate(pairs)]
    for cp in ins:
        cp.start()
    for a, b in zip(ins, outs):
        a.wait()
        b.start()
    for cp in outs:
        cp.wait()


def body(tokens, cotangent, norm_gain, row_prev, col_prev):
    hbm = pl.BlockSpec(memory_space=pl.ANY)
    u, r, c = call(CFG, 0, "adafactor", tokens, cotangent, norm_gain, row_prev, col_prev)
    u, r, c = pl.pallas_call(
        write,
        out_shape=tuple(jax.ShapeDtypeStruct(a.shape, F32) for a in (u, r, c)),
        in_specs=[hbm] * 3,
        out_specs=(hbm,) * 3,
        scratch_shapes=[
            pltpu.VMEM((ROWS, WIDE), F32),
            pltpu.VMEM((1, ROWS), F32),
            pltpu.VMEM((1, WIDE), F32),
            pltpu.SemaphoreType.DMA((6,)),
            pltpu.SemaphoreType.DMA((6,)),
        ],
        compiler_params=pltpu.CompilerParams(vmem_limit_bytes=60 << 20),
        name="write",
    )(u, r, c)
    return u[None], r, c[0]


CFG = {"zf": 384, "zs": 1, "ys": 1}


def solution(mesh):
    return jax.shard_map(
        body,
        mesh=mesh,
        in_specs=(
            P(("cuts", "dp"), "row"),
            P(("cuts", "dp"), "col"),
            P("row"),
            P("row", "dp"),
            P("col"),
        ),
        out_specs=(P("row", "dp", "col"), P("row", "dp"), P("col")),
        check_vma=False,
    )
```

```python
import functools

import jax
import jax.numpy as jnp
from jax import lax
from jax.experimental import pallas as pl
from jax.experimental.pallas import tpu as pltpu
from jax.sharding import PartitionSpec as P

MESH = pl.DeviceIdType.MESH
F32 = jnp.float32

D = 4096
F = 4096
DECAY = 0.975
EPS = 1e-30
CLIP = 1.0

NZ, NROW, NCOL, NCUT = 16, 4, 4, 2
N8 = NROW * NCUT
N32 = NCOL * N8
ROWS = 64
HALF = 32
WIDE = 1024


def make_chunks(cfg):
    zf, zs, yk = cfg["zf"], cfg["zs"], cfg["ys"]
    z, y = [], []
    for theirs in (1, 0):
        for q in range(zs):
            z.append((0, theirs, 0, HALF, q * (zf // zs), zf // zs, (1 - theirs + q) % 2))
    yw = (WIDE - zf) // yk
    for q in range(yk):
        for r in range(2):
            y.append((1, 0, r * 16, 16, zf + q * yw, yw, (r + q) % 2))
    return z, y


def kernel(cfg, *refs):
    zc, yc = make_chunks(cfg)
    chunks = zc + yc
    nch = len(chunks)
    zf = cfg["zf"]
    (x_hbm, c_hbm, gain_hbm, rprev_hbm, cprev_hbm, upd_hbm, rmom_hbm, cmom_hbm,
     upd_ref, rmom_ref, cmom_ref, out_sem,
     x_ref, c_ref, gain_ref, rprev_ref, cprev_ref, part) = refs[:18]
    rbufs = refs[18:18 + nch]
    (ybuf, zx_src, zx_dst, gfull, rr, rx_src, rx_dst, ab_src, ab, zab, fin,
     in_sem, ssem, rsem, ys, yr, zxs, zxr, gs, gr, rs, rrs, rxs, rxr, abs_, abr, zs, zr, fs, fr,
     ) = refs[18 + nch:]
    d = lax.axis_index("dp")
    c = lax.axis_index("cuts")
    row = lax.axis_index("row")
    col = lax.axis_index("col")
    other = 1 - c
    me8 = row * NCUT + c
    me32 = col * N8 + me8
    up = {"dp": lax.rem(d + 1, NZ)}
    down = {"dp": lax.rem(d + NZ - 1, NZ)}
    pair = {"cuts": other}

    rows4 = [lax.rem(row + k, NROW) for k in range(NROW)]
    cols4 = [lax.rem(col + k, NCOL) for k in range(NCOL)]
    cuts2 = [c, other]

    group = [
        (rows4[a] * NCUT + cuts2[b], {"row": rows4[a], "cuts": cuts2[b]})
        for a in range(NROW) for b in range(NCUT) if a or b
    ]
    plane = [
        (cols4[k] * N8 + rows4[a] * NCUT + cuts2[b], {"col": cols4[k], "row": rows4[a], "cuts": cuts2[b]})
        for k in (2, 1, 3, 0) for a in (2, 1, 3, 0) for b in (1, 0) if k or a or b
    ]

    def remote(src, dst, s, r, dev):
        return pltpu.make_async_remote_copy(
            src_ref=src, dst_ref=dst, send_sem=s, recv_sem=r,
            device_id=dev, device_id_type=MESH,
        )

    barrier = pltpu.get_barrier_semaphore()

    def greet(dev):
        pl.semaphore_signal(barrier, inc=1, device_id=dev, device_id_type=MESH)

    def upper(j):
        return lax.rem(j + d, 2)

    def block(j):
        return lax.rem(d // 2 + 12 + (1 - 2 * upper(j)) * ((j + 1) // 2), 8)

    def x_load(j):
        at = pl.ds(pl.multiple_of(block(j) * 128, 128), 128)
        return pltpu.make_async_copy(x_hbm.at[:, at], x_ref.at[:, at], in_sem.at[j])

    c_loads = [
        pltpu.make_async_copy(c_hbm.at[pl.ds(n * 128, 128)], c_ref.at[pl.ds(n * 128, 128)], in_sem.at[8 + n])
        for n in range(8)
    ]
    small_loads = [
        pltpu.make_async_copy(a, b, in_sem.at[16 + n])
        for n, (a, b) in enumerate([
            (gain_hbm, gain_ref), (rprev_hbm, rprev_ref), (cprev_hbm, cprev_ref),
        ])
    ]
    x_load(0).start()
    for load in c_loads:
        load.start()
    greet(up)
    greet(down)
    for _, dev in group:
        greet(dev)
    for k in range(1, NCOL):
        greet({"col": cols4[k]})
    for j in range(1, 4):
        x_load(j).start()
    for load in c_loads:
        load.wait()
    for j in range(4, 8):
        x_load(j).start()
    for load in small_loads:
        load.start()

    def product(j):
        at = pl.ds(pl.multiple_of(block(j) * 128, 128), 128)
        x_load(j).wait()
        part[at, :] = lax.dot_general(
            x_ref[:, at], c_ref[...], (((0,), (0,)), ((), ())),
            preferred_element_type=F32,
        )

    def y_copy(e):
        rows_ = pl.ds(pl.multiple_of(e * ROWS + other * HALF, HALF), HALF)
        return remote(part.at[rows_, pl.ds(zf, WIDE - zf)], ybuf.at[e], ys.at[e], yr.at[e], pair)

    def y_send(j):
        p = block(j)
        y_copy(2 * p + upper(j)).start()
        y_copy(2 * p + 1 - upper(j)).start()

    def first(j, _):
        product(j)
        return 0

    def later(j, _):
        product(j)
        y_send(j)
        return 0

    def own(e, chunk):
        _, theirs, r0, nr, c0, w, _ = chunk
        h = other if theirs else c
        return part.at[pl.ds(pl.multiple_of(e * ROWS + h * HALF + r0, nr), nr), pl.ds(c0, w)]

    def dest(direction, distance):
        return lax.rem(d + (NZ - distance if direction else distance), NZ)

    def hop(direction, n, i, src):
        ch = direction * nch + n
        return remote(
            src, rbufs[n].at[direction, i], ssem.at[ch, i], rsem.at[ch, i],
            {"dp": dest(direction, 1)},
        )

    def begin(direction, n, i):
        hop(direction, n, i, own(dest(direction, 8 - i), chunks[n])).start()

    def forward(direction, n, i):
        slot = rbufs[n].at[direction, i - 1]
        hop(direction, n, i - 1, slot).wait_recv()
        slot[...] += own(dest(direction, 8 - i), chunks[n])[...]
        hop(direction, n, i, slot).start()

    def y_add(e):
        y_copy(e).wait_recv()
        rows_ = pl.ds(pl.multiple_of(e * ROWS + c * HALF, HALF), HALF)
        part[rows_, pl.ds(zf, WIDE - zf)] += ybuf[e]

    zn = range(len(zc))
    yn = range(len(zc), nch)

    def start0(which_n):
        for n in which_n:
            begin(chunks[n][6], n, 0)

    def start1(which_n):
        for n in which_n:
            begin(1 - chunks[n][6], n, 1)

    def second(which_n):
        for n in which_n:
            forward(chunks[n][6], n, 1)

    def z_step(i):
        for ahead in (1, 0):
            for n in zn:
                forward(chunks[n][6] ^ ahead, n, i)

    def y_step(i):
        for direction in (0, 1):
            y_add(dest(direction, 8 - i))
        for ahead in (1, 0):
            for n in yn:
                forward(chunks[n][6] ^ ahead, n, i)

    def fill(j, _):
        product(j)

        @pl.when(j == 0)
        def _():
            pl.semaphore_wait(barrier, 2 + (N8 - 1) + (NCOL - 1))
            start0(zn)

        y_send(j)

        @pl.when(j == 1)
        def _():
            start1(zn)

        @pl.when(j == 6)
        def _():
            second(zn)

        return 0

    lax.fori_loop(0, 8, fill, 0)
    for load in small_loads:
        load.wait()
    y_add(dest(0, 8))
    start0(yn)
    z_step(2)
    for direction in (0, 1):
        y_add(dest(direction, 7))
    start1(yn)
    second(yn)

    def steps(i, _):
        z_step(i)
        y_step(i - 1)
        return 0

    lax.fori_loop(3, 8, steps, 0)

    def collect(n):
        for direction in (0, 1):
            hop(direction, n, 7, rbufs[n].at[direction, 7]).wait_recv()
        return own(d, chunks[n])[...] + rbufs[n][0, 7] + rbufs[n][1, 7]

    for n in zn:
        _, theirs, r0, nr, c0, w, _ = chunks[n]
        if theirs:
            zx_src[:, pl.ds(c0, w)] = collect(n)
    zx = remote(zx_src, zx_dst, zxs, zxr, pair)
    zx.start()
    y_step(7)
    y_add(d)

    lane = lax.broadcasted_iota(jnp.int32, (HALF, WIDE), 1)
    sub = lax.broadcasted_iota(jnp.int32, (HALF, WIDE), 0)
    gain = jnp.sum(
        jnp.where(lane == sub + d * ROWS + c * HALF, gain_ref[...], 0.0), axis=1, keepdims=True
    )
    mine = pl.ds(pl.multiple_of(c * HALF, HALF), HALF)
    for n in zn:
        _, theirs, r0, nr, c0, w, _ = chunks[n]
        if not theirs:
            gfull[mine, pl.ds(c0, w)] = collect(n)
    zx.wait_recv()
    gfull[mine, pl.ds(0, zf)] += zx_dst[...]
    for n in yn:
        _, theirs, r0, nr, c0, w, _ = chunks[n]
        gfull[pl.ds(pl.multiple_of(c * HALF + r0, nr), nr), pl.ds(c0, w)] = collect(n)
    g = gfull[mine, :] * gain
    gfull[mine, :] = g
    g_copy = remote(gfull.at[mine], gfull.at[mine], gs, gr, pair)

    lane1 = lax.broadcasted_iota(jnp.int32, (HALF, 128), 1)
    sub1 = lax.broadcasted_iota(jnp.int32, (HALF, 128), 0)
    diag = lane1 == sub1 + c * HALF
    sq = g * g
    rsum = jnp.sum(sq, axis=1, keepdims=True)
    rr[col] = jnp.sum(jnp.where(diag, rsum, 0.0), axis=0, keepdims=True)
    rcopies = []
    for k in range(1, NCOL):
        to = cols4[k]
        cp = remote(rr.at[col], rr.at[col], rs.at[k], rrs.at[col], {"col": to})
        cp.start()
        rcopies.append(cp)
    g_copy.start()
    asum = jnp.sum(sq, axis=0, keepdims=True)
    for e in range(N8):
        ab_src[e, :, pl.ds(0, 128)] = asum[:, e * 128:(e + 1) * 128]
    for k in range(1, NCOL):
        frm = cols4[k]
        remote(rr.at[frm], rr.at[frm], rs.at[k], rrs.at[frm], {"col": frm}).wait_recv()
    total = rr[0] + rr[1] + rr[2] + rr[3]
    lane_r = lax.broadcasted_iota(jnp.int32, (1, 128), 1)
    in_half = (lane_r >= c * HALF) & (lane_r < c * HALF + HALF)
    rprev = jnp.concatenate([rprev_ref[...], rprev_ref[...]], axis=1)
    rmom = DECAY * rprev + (1.0 - DECAY) * (total / F + EPS)
    rmom = jnp.where(in_half, rmom, 0.0)
    rcol = jnp.sum(jnp.where(diag, rmom, 0.0), axis=1, keepdims=True)
    bsum = jnp.sum(sq * (1.0 / rcol), axis=0, keepdims=True)
    for e in range(N8):
        ab_src[e, :, pl.ds(128, 128)] = bsum[:, e * 128:(e + 1) * 128]

    acopies = []
    for k, (e, dev) in enumerate(group):
        cp = remote(ab_src.at[e], ab.at[me8], abs_.at[k], abr.at[me8], dev)
        cp.start()
        acopies.append(cp)
    rx_src[...] = rmom
    rx = remote(rx_src, rx_dst, rxs, rxr, pair)
    rx.start()
    ab[me8] = ab_src[me8]
    for k, (e, dev) in enumerate(group):
        remote(ab_src.at[e], ab.at[e], abs_.at[k], abr.at[e], dev).wait_recv()
    acc = ab[0]
    for e in range(1, N8):
        acc = acc + ab[e]

    zab[d] = acc
    zcopies = []
    order = [8] + [k for m in range(7, 0, -1) for k in (m, 16 - m)]
    for k in order:
        to = lax.rem(d + k, NZ)
        cp = remote(zab.at[d], zab.at[d], zs.at[k], zr.at[d], {"dp": to})
        cp.start()
        zcopies.append(cp)
    cprev = cprev_ref[:, pl.ds(pl.multiple_of(me8 * 128, 128), 128)]
    for k in reversed(order):
        frm = lax.rem(d + k, NZ)
        remote(zab.at[frm], zab.at[frm], zs.at[k], zr.at[frm], {"dp": frm}).wait_recv()
    acc = zab[0]
    for e in range(1, NZ):
        acc = acc + zab[e]
    cmom = DECAY * cprev + (1.0 - DECAY) * (acc[:, 0:128] / D + EPS)
    fin[me32, :, pl.ds(0, 128)] = cmom
    fin[me32, :, pl.ds(128, 128)] = acc[:, 128:256] / cmom

    fcopies = []
    for k, (_, dev) in enumerate(plane):
        cp = remote(fin.at[me32], fin.at[me32], fs.at[k], fr.at[me32], dev)
        cp.start()
        fcopies.append(cp)

    rx.wait_recv()
    rfull = rmom + rx_dst[...]
    rmom_ref[...] = rfull[:, 0:ROWS]
    outs = [pltpu.make_async_copy(rmom_ref, rmom_hbm, out_sem.at[N8])]
    outs[0].start()
    lane2 = lax.broadcasted_iota(jnp.int32, (ROWS, 128), 1)
    sub2 = lax.broadcasted_iota(jnp.int32, (ROWS, 128), 0)
    rscale = lax.rsqrt(jnp.sum(jnp.where(lane2 == sub2, rfull, 0.0), axis=1, keepdims=True))
    g_copy.wait_recv()

    for n in range(nch):
        for direction in (0, 1):
            lo = 0 if direction == chunks[n][6] else 1

            def drain(i, _, direction=direction, n=n):
                hop(direction, n, i, rbufs[n].at[direction, i]).wait_send()
                return 0

            lax.fori_loop(lo, 8, drain, 0)

    def drain_y(e, _):
        y_copy(e).wait_send()
        return 0

    lax.fori_loop(0, NZ, drain_y, 0)
    zx.wait_send()
    g_copy.wait_send()
    rx.wait_send()
    for cp in rcopies + acopies + zcopies:
        cp.wait_send()

    for k, (e, dev) in enumerate(plane):
        remote(fin.at[e], fin.at[e], fs.at[k], fr.at[e], dev).wait_recv()
    tot = fin[0, :, pl.ds(128, 128)]
    for e in range(1, N32):
        tot = tot + fin[e, :, pl.ds(128, 128)]
    ratio = jnp.sum(tot, axis=1, keepdims=True) / (D * F)
    inverse = 1.0 / jnp.maximum(1.0, jnp.sqrt(ratio) / CLIP)
    rows_scale = rscale * inverse
    for e in range(N8):
        at = pl.ds(e * 128, 128)
        cm = fin[col * N8 + e, :, pl.ds(0, 128)]
        cmom_ref[:, at] = cm
        upd_ref[:, at] = gfull[:, at] * rows_scale * lax.rsqrt(cm)
        outs.append(pltpu.make_async_copy(upd_ref.at[:, at], upd_hbm.at[:, at], out_sem.at[e]))
        outs[-1].start()
    outs.append(pltpu.make_async_copy(cmom_ref, cmom_hbm, out_sem.at[N8 + 1]))
    outs[-1].start()
    for cp in fcopies:
        cp.wait_send()
    for cp in outs:
        cp.wait()


def call(cfg, cid, name, tokens, cotangent, norm_gain, row_prev, col_prev):
    zc, yc = make_chunks(cfg)
    chunks = zc + yc
    nch = len(chunks)
    zf = cfg["zf"]
    hbm = pl.BlockSpec(memory_space=pl.ANY)
    dma = pltpu.SemaphoreType.DMA
    bf = jnp.bfloat16
    return pl.pallas_call(
        functools.partial(kernel, cfg),
        out_shape=(
            jax.ShapeDtypeStruct((ROWS, WIDE), F32),
            jax.ShapeDtypeStruct((1, ROWS), F32),
            jax.ShapeDtypeStruct((1, WIDE), F32),
        ),
        in_specs=[hbm] * 5,
        out_specs=(hbm, hbm, hbm),
        scratch_shapes=[
            pltpu.VMEM((ROWS, WIDE), F32),
            pltpu.VMEM((1, ROWS), F32),
            pltpu.VMEM((1, WIDE), F32),
            dma((N8 + 2,)),
            pltpu.VMEM((1024, 1024), bf),
            pltpu.VMEM((1024, 1024), bf),
            pltpu.VMEM((1, 1024), F32),
            pltpu.VMEM((1, ROWS), F32),
            pltpu.VMEM((1, WIDE), F32),
            pltpu.VMEM((1024, WIDE), F32),
        ] + [pltpu.VMEM((2, 8, ch[3], ch[5]), F32) for ch in chunks] + [
            pltpu.VMEM((NZ, HALF, WIDE - zf), F32),
            pltpu.VMEM((HALF, zf), F32),
            pltpu.VMEM((HALF, zf), F32),
            pltpu.VMEM((ROWS, WIDE), F32),
            pltpu.VMEM((NCOL, 1, 128), F32),
            pltpu.VMEM((1, 128), F32),
            pltpu.VMEM((1, 128), F32),
            pltpu.VMEM((N8, 1, 256), F32),
            pltpu.VMEM((N8, 1, 256), F32),
            pltpu.VMEM((NZ, 1, 256), F32),
            pltpu.VMEM((N32, 1, 256), F32),
            dma((19,)),
            dma((2 * nch, 8)), dma((2 * nch, 8)),
            dma((NZ,)), dma((NZ,)),
            dma, dma, dma, dma,
            dma((NCOL,)), dma((NCOL,)),
            dma, dma,
            dma((N8,)), dma((N8,)),
            dma((NZ,)), dma((NZ,)),
            dma((N32,)), dma((N32,)),
        ],
        compiler_params=pltpu.CompilerParams(
            collective_id=cid, has_side_effects=True, vmem_limit_bytes=56 << 20
        ),
        name=name,
    )(tokens, cotangent, norm_gain[None, :], row_prev, col_prev[None, :])


def write(u, r, c, uo, ro, co, uv, rv, cv, isem, osem):
    pieces = 4
    rows_ = [pl.ds(n * (ROWS // pieces), ROWS // pieces) for n in range(pieces)]
    pairs = [(u.at[at], uv.at[at], uo.at[at]) for at in rows_] + [(r, rv, ro), (c, cv, co)]
    ins = [pltpu.make_async_copy(a, b, isem.at[n]) for n, (a, b, _) in enumerate(pairs)]
    outs = [pltpu.make_async_copy(b, o, osem.at[n]) for n, (_, b, o) in enumerate(pairs)]
    for cp in ins:
        cp.start()
    for a, b in zip(ins, outs):
        a.wait()
        b.start()
    for cp in outs:
        cp.wait()


def body(tokens, cotangent, norm_gain, row_prev, col_prev):
    hbm = pl.BlockSpec(memory_space=pl.ANY)
    u, r, c = call(CFG, 0, "adafactor", tokens, cotangent, norm_gain, row_prev, col_prev)
    u, r, c = pl.pallas_call(
        write,
        out_shape=tuple(jax.ShapeDtypeStruct(a.shape, F32) for a in (u, r, c)),
        in_specs=[hbm] * 3,
        out_specs=(hbm,) * 3,
        scratch_shapes=[
            pltpu.VMEM((ROWS, WIDE), F32),
            pltpu.VMEM((1, ROWS), F32),
            pltpu.VMEM((1, WIDE), F32),
            pltpu.SemaphoreType.DMA((6,)),
            pltpu.SemaphoreType.DMA((6,)),
        ],
        compiler_params=pltpu.CompilerParams(vmem_limit_bytes=60 << 20),
        name="write",
    )(u, r, c)
    return u[None], r, c[0]


CFG = {"zf": 384, "zs": 1, "ys": 1}


def solution(mesh):
    return jax.shard_map(
        body,
        mesh=mesh,
        in_specs=(
            P(("cuts", "dp"), "row"),
            P(("cuts", "dp"), "col"),
            P("row"),
            P("row", "dp"),
            P("col"),
        ),
        out_specs=(P("row", "dp", "col"), P("row", "dp"), P("col")),
        check_vma=False,
    )
```
